256 devices in a mesh: gx: 4 (over x), gy: 16 (over z, y_lo), gz: 4 (over y_hi, core).
Axes of the slice: x: 4, y: 4 (y_hi: 2, y_lo: 2; y = y_hi * 2 + y_lo), z: 8, core: 2. Of those that a mesh axis runs over, the one named last changes fastest.
Arguments:
- adjoint_state: float32 [8, 16, 8, 125, 128], P('gx', 'gy', 'gz'), may hold values from -6 to 6
- bulk_modulus: float32 [8, 16, 8], P('gx', 'gy', 'gz'), may hold values from 0.5 to 2
- buoyancy: float32 [8, 16, 8], P('gx', 'gy', 'gz'), may hold values from 0.5 to 2
- water_layers: int32 [8, 16], P('gx', 'gy'), may hold values from 1 to 8
- surface_cell: int32 [8, 16], P('gx', 'gy'), may hold values from 0 to 511, as said below
Outputs:
- adjoint_state_out: float32 [8, 16, 8, 125, 128], P('gx', 'gy', 'gz')
- seafloor_trace: float32 [512, 25, 128], P(('gx', 'gy'))
The draws below stay inside these ranges and needn't reach their ends.
Inputs may be any that keep to these rules, and one draw needn't show every extreme that they name: `surface_cell`: the owner of cell c is c // 8 along gx+gy (flat index, gx slowest). The seafloor faces of the 2 x 1 element columns of one device name only owners at flat offsets 0 to 3 from that device's own flat index, taken modulo the number of owners; each owner that is named is named exactly 2 times by that device.
All inputs are finite; a program needn't handle non-finite values.
Results may differ from the reference program's by a relative error of at most 0.0001.
Values sent between devices are 32-bit elements; how exact they have to be, the bound alone decides.
A program may use at most 64 MiB of HBM per device.

```python
import math
import jax
import jax.numpy as jnp
import numpy as np
from jax import lax

FIELDS = 4
COLS = 32
STEPS = 2
CAP = 2
NEAR = 4
EX = 2
EY = 1
S_DEV = 8
NXE = 8
NYE = 16
NZE = 8
SURF = 512
N_GX = 4
N_GY = 16


def draw_surface_cell(key, part):
    key = jax.random.fold_in(key, 11)
    owners = N_GX * N_GY
    face_count = EX * EY
    key_perm, key_order, key_cell = jax.random.split(key, 3)
    offset_order = jax.vmap(lambda sub_key: jax.random.permutation(sub_key, NEAR))(jax.random.split(key_perm, owners))
    owner_rows = jnp.arange(owners)[:, None]
    edge_rows = (owner_rows == 0) | (owner_rows == owners - 1)
    relabelled = (offset_order - offset_order[:, :1]) % NEAR
    offset_order = jnp.where(edge_rows, relabelled, offset_order)
    face_pos = jnp.arange(face_count)
    offsets_named = offset_order[:, face_pos // CAP]
    shuffle = jax.vmap(lambda sub_key: jax.random.permutation(sub_key, face_count))(jax.random.split(key_order, owners))
    offsets_named = jnp.take_along_axis(offsets_named, shuffle, axis=1)
    owner_face = (owner_rows + offsets_named) % owners
    cell_offsets = jax.random.randint(key_cell, (owners, face_count), 0, S_DEV)
    first_edge = (owner_rows == 0) & (owner_face == 0)
    last_edge = (owner_rows == owners - 1) & (owner_face == owners - 1)
    cell_offsets = jnp.where(first_edge, 0, cell_offsets)
    cell_offsets = jnp.where(last_edge, S_DEV - 1, cell_offsets)
    cell_ids = owner_face * S_DEV + cell_offsets
    cell_ids = cell_ids.reshape(N_GX, N_GY, EX, EY).transpose(0, 2, 1, 3).reshape(EX * N_GX, EY * N_GY)
    return cell_ids.astype(jnp.int32)


def plant(result, own_key, low, top_value):
    place = [jax.random.randint(jax.random.fold_in(own_key, axis), (), 0, length) for axis, length in enumerate(result.shape)]
    widest = result.shape.index(max(result.shape))
    beside = place[:widest] + [(place[widest] + 1) % result.shape[widest]] + place[widest + 1:]
    return result.at[tuple(place)].set(low).at[tuple(beside)].set(top_value)


def steps_of(own_key, dims, cuts, low, high):
    gain, own = 1.0, jax.random.fold_in(own_key, 6)
    for axis_at, parts in cuts:
        draws = jnp.exp(jax.random.uniform(jax.random.fold_in(own, axis_at), (parts,), jnp.float32, low / len(cuts), high / len(cuts)))
        gain = gain * jnp.repeat(draws, dims[axis_at] // parts).reshape([-1 if axis == axis_at else 1 for axis in range(len(dims))])
    return gain


def gaussian(stream_key, extent, scale, bound, pieces=(), held_as=jnp.bfloat16):
    factor_of = steps_of(stream_key, extent, pieces, -0.22, 0.18) if pieces else 1.0
    drawn = jax.random.normal(stream_key, extent, jnp.float32) * scale * factor_of
    return jnp.minimum(jnp.maximum(drawn, -bound), bound).astype(held_as)


def setup_inputs(seed: int = 0) -> dict:
    keys = jax.random.split(jax.random.key(seed), 6)
    return {
        "adjoint_state": gaussian(keys[0], (NXE, NYE, NZE, 125, FIELDS * COLS), 1.0, 6.0, ((0, 4), (1, 16), (2, 4)), jnp.float32),
        "bulk_modulus": jnp.clip(jnp.exp(math.log(2.0) - 1.3862944 * jax.random.uniform(keys[1], (NXE, NYE, NZE), jnp.float32) ** steps_of(keys[1], (NXE, NYE, NZE), ((0, 4), (1, 16), (2, 4)), -0.2, 0.2)), 0.5, 2.0),
        "buoyancy": jnp.clip(jnp.exp(math.log(2.0) - 1.3862944 * jax.random.uniform(keys[2], (NXE, NYE, NZE), jnp.float32) ** steps_of(keys[2], (NXE, NYE, NZE), ((0, 4), (1, 16), (2, 4)), -0.2, 0.2)), 0.5, 2.0),
        "water_layers": plant(jax.random.randint(keys[3], (NXE, NYE), 1, NZE + 1), jax.random.fold_in(keys[3], 1), 1, NZE).astype(jnp.int32),
        "surface_cell": draw_surface_cell(jax.random.fold_in(keys[5], 71), 0),
    }


lift_gain = 10.0
gravity_term = 2.0
time_step = 0.02
section_weights = (1.0 / 6.0, 1.0 / 3.0, 1.0 / 3.0, 1.0 / 6.0)
einsum_forms = ('ia,xyzabcf->xyzibcf', 'ib,xyzabcf->xyzaicf', 'ic,xyzabcf->xyzabif')

def derivative_table():
    points = np.array([-1.0, -math.sqrt(3.0 / 7.0), 0.0, math.sqrt(3.0 / 7.0), 1.0])
    scales = np.array([np.prod([points[node_row] - points[other_node] for other_node in range(5) if other_node != node_row]) for node_row in range(5)])
    deriv_table = np.zeros((5, 5))
    for node_row in range(5):
        for node_col in range(5):
            if node_row != node_col:
                deriv_table[node_row, node_col] = scales[node_row] / scales[node_col] / (points[node_row] - points[node_col])
        deriv_table[node_row, node_row] = -np.sum(deriv_table[node_row])
    return jnp.asarray(deriv_table, dtype=jnp.float32)

def directional(field_state, deriv_table, axis_d):
    return jnp.einsum(einsum_forms[axis_d], deriv_table, field_state, precision=lax.Precision.HIGHEST)

def face_correction(inner, outer, bulk_in, buoy_in, bulk_out, buoy_out, normal_sign, axis_d, columns):
    offset = (1 + axis_d) * columns
    pressure_in = inner[..., :columns]
    pressure_out = outer[..., :columns]
    velocity_in = inner[..., offset:offset + columns]
    velocity_out = outer[..., offset:offset + columns]
    wave_speed = jnp.maximum(jnp.sqrt(bulk_in * buoy_in), jnp.sqrt(bulk_out * buoy_out))
    penalty = -0.5 * wave_speed * (inner - outer)
    pressure_jump = 0.5 * normal_sign * (buoy_out * velocity_out - buoy_in * velocity_in)
    velocity_jump = 0.5 * normal_sign * (bulk_out * pressure_out - bulk_in * pressure_in)
    zeros_block = jnp.zeros_like(pressure_jump)
    blocks = [pressure_jump, zeros_block, zeros_block, zeros_block]
    blocks[1 + axis_d] = velocity_jump
    return lift_gain * (penalty + jnp.concatenate(blocks, axis=-1))

def shift_along(values, axis, amount):
    pad_width = [(0, 0)] * values.ndim
    length = values.shape[axis]
    if amount > 0:
        pad_width[axis] = (1, 0)
        padded = jnp.pad(values, pad_width)
        return lax.slice_in_dim(padded, 0, length, axis=axis)
    pad_width[axis] = (0, 1)
    padded = jnp.pad(values, pad_width)
    return lax.slice_in_dim(padded, 1, length + 1, axis=axis)

def tendency(field_state, bulk_face, buoy_face, active, deriv_table):
    columns = field_state.shape[-1] // 4
    bulk_cell = bulk_face[..., None]
    buoy_cell = buoy_face[..., None]
    pressure = field_state[..., :columns]
    pressure_rate = jnp.zeros_like(pressure)
    velocity_rates = []
    for axis_d in range(3):
        slope = directional(field_state, deriv_table, axis_d)
        offset = (1 + axis_d) * columns
        pressure_rate = pressure_rate + buoy_cell * slope[..., offset:offset + columns]
        velocity_rate = bulk_cell * slope[..., :columns]
        if axis_d == 2:
            velocity_rate = velocity_rate + gravity_term / buoy_cell * pressure
        velocity_rates.append(velocity_rate)
    tendency_now = jnp.concatenate([pressure_rate] + velocity_rates, axis=-1)
    for axis_d in range(3):
        node_axis = 3 + axis_d
        lower = lax.index_in_dim(field_state, 0, node_axis, keepdims=False)
        upper = lax.index_in_dim(field_state, 4, node_axis, keepdims=False)
        below = shift_along(upper, axis_d, 1)
        above = shift_along(lower, axis_d, -1)
        low_term = face_correction(lower, below, bulk_face, buoy_face, shift_along(bulk_face, axis_d, 1), shift_along(buoy_face, axis_d, 1), -1.0, axis_d, columns)
        high_term = face_correction(upper, above, bulk_face, buoy_face, shift_along(bulk_face, axis_d, -1), shift_along(buoy_face, axis_d, -1), 1.0, axis_d, columns)
        leading = (slice(None),) * node_axis
        tendency_now = tendency_now.at[leading + (0,)].add(low_term)
        tendency_now = tendency_now.at[leading + (4,)].add(high_term)
    return tendency_now * active

def reference(adjoint_state, bulk_modulus, buoyancy, water_layers, surface_cell):
    deriv_table = derivative_table()
    count_x, count_y, count_z = bulk_modulus.shape
    width = adjoint_state.shape[-1]
    depth_index = jnp.arange(count_z, dtype=jnp.int32)
    active = (depth_index[None, None, :] < water_layers[:, :, None]).astype(jnp.float32)[..., None, None, None, None]
    field_state = adjoint_state.reshape(count_x, count_y, count_z, 5, 5, 5, width) * active
    select = (depth_index[None, None, :] == (water_layers - 1)[:, :, None]).astype(jnp.float32)[..., None, None, None]
    bulk_face = bulk_modulus[..., None, None, None]
    buoy_face = buoyancy[..., None, None, None]
    floor_sum = jnp.zeros((count_x, count_y, 5, 5, width), jnp.float32)
    for step_index in range(STEPS):
        section_input = field_state
        update = field_state
        for section_no in range(4):
            bottom = lax.optimization_barrier(jnp.sum(select * section_input[:, :, :, :, :, 4, :], axis=2))
            floor_sum = floor_sum + time_step * section_weights[section_no] * bottom
            tendency_now = tendency(section_input, bulk_face, buoy_face, active, deriv_table)
            if section_no == 0:
                update = tendency_now
            elif section_no < 3:
                update = update + 2.0 * tendency_now
            else:
                update = update + tendency_now
            if section_no < 2:
                section_input = field_state + time_step * 0.5 * tendency_now
            elif section_no == 2:
                section_input = field_state + time_step * tendency_now
        field_state = field_state + time_step / 6.0 * update
    cell_ids = surface_cell.reshape(-1)
    surface_sums = jax.ops.segment_sum(floor_sum.reshape(count_x * count_y, 25 * width), cell_ids, num_segments=SURF)
    return (field_state.reshape(count_x, count_y, count_z, 125, width), surface_sums.reshape(SURF, 25, width))
```

```python
import math

import jax
import jax.numpy as jnp
import numpy as np
from jax import lax
from jax.experimental import pallas as pl
from jax.experimental.pallas import tpu as pltpu
from jax.sharding import PartitionSpec as P

N_GX = 4
N_GZ = 4
N_ZC = 8
SECTIONS = 8
S_DEV = 8
GRAVITY = 2.0
DT = 0.02
MESH = pl.DeviceIdType.MESH


def derivative_rows():
    points = np.array([-1.0, -math.sqrt(3.0 / 7.0), 0.0, math.sqrt(3.0 / 7.0), 1.0])
    scales = np.array(
        [np.prod([points[a] - points[b] for b in range(5) if b != a]) for a in range(5)]
    )
    table = np.zeros((5, 5))
    for a in range(5):
        for b in range(5):
            if a != b:
                table[a, b] = scales[a] / scales[b] / (points[a] - points[b])
        table[a, a] = -np.sum(table[a])
    table[0, 0] += 5.0
    table[4, 4] -= 5.0
    table[np.abs(table) < 1e-12] = 0.0
    return table


TABLE = derivative_rows()


def weighted(row, parts):
    total = None
    for weight, part in zip(row, parts):
        if weight != 0.0:
            term = float(weight) * part
            total = term if total is None else total + term
    return total


def bit_mask(shape, bit):
    lanes = lax.broadcasted_iota(jnp.int32, shape, len(shape) - 1)
    return (lanes & (1 << bit)) != 0


def lane_roll(value, shift):
    return pltpu.roll(value, shift % 128, axis=value.ndim - 1)


def swap_pair(low, high, bit):
    width = 1 << bit
    mask = bit_mask(low.shape, bit)
    return (
        jnp.where(mask, lane_roll(high, width), low),
        jnp.where(mask, high, lane_roll(low, -width)),
    )


def swap_bits(blocks, pairs):
    blocks = list(blocks)
    for index_bit, lane_bit in pairs:
        step = 1 << index_bit
        for at in range(len(blocks)):
            if not at & step:
                blocks[at], blocks[at + step] = swap_pair(blocks[at], blocks[at + step], lane_bit)
    return blocks


def flip(value, bit):
    width = 1 << bit
    mask = bit_mask(value.shape, bit)
    return jnp.where(mask, lane_roll(value, width), lane_roll(value, -width))


def fold_pair(low, high, bit):
    mask = bit_mask(low.shape, bit)
    return jnp.where(mask, high, low) + flip(jnp.where(mask, low, high), bit)


def fold_bits(blocks, bits):
    for bit in bits:
        blocks = [fold_pair(blocks[at], blocks[at + 1], bit) for at in range(0, len(blocks), 2)]
    return blocks[0]


FIELD_BITS = ((0, 5), (1, 6))
RANK_BITS = ((0, 2), (1, 3), (2, 4))

VOL_B, VOL_K, VOL_G, ACTIVE, COL_D = 0, 1, 2, 3, 4
INNER = 9
OUTER = 21
Z_ROWS = 37
SELECT = 45
BULK, BUOY, SPEED = 46, 47, 48
N_COEF = 49


def face_of(direction):
    axis, side = direction // 2, direction % 2
    bit = 6 if axis == 0 else 4
    width = 1 << bit
    return axis, side, bit, (width if side == 1 else -width)


def kernel(
    state_hbm, bulk, buoy, layers, cells, out_hbm, trace_hbm,
    staged, nat, pack_out, pack_in, back_out, back_in, state, base, update, rate, coef,
    face_out, face_in, floor, tr_out, tr_in, tb_out, tb_in, trace,
    local_sem, a_send, a_recv, h_send, h_recv, t_send, t_recv, b_send, b_recv, c_send, c_recv,
):
    gx = lax.axis_index("gx")
    gy = lax.axis_index("gy")
    gz = lax.axis_index("gz")
    zc, y_lo = gy // 2, gy % 2
    y_hi, core = gz // 2, gz % 2
    me = y_lo * 4 + y_hi * 2 + core

    load = pltpu.make_async_copy(state_hbm, staged, local_sem.at[0])
    load.start()

    def partner(delta):
        to_y = 1 - y_lo if delta & 4 else y_lo
        to_h = 1 - y_hi if delta & 2 else y_hi
        to_c = 1 - core if delta & 1 else core
        return (gx, zc * 2 + to_y, to_h * 2 + to_c), to_y * 4 + to_h * 2 + to_c, to_y

    def along(steps):
        flat = (gx * N_ZC + zc + steps + N_GX * N_ZC) % (N_GX * N_ZC)
        return (flat // N_ZC, (flat % N_ZC) * 2 + y_lo, gz)

    neighbours = [
        ((gx + N_GX - 1) % N_GX, gy, gz),
        ((gx + 1) % N_GX, gy, gz),
        (gx, (gy + 2 * N_ZC - 2) % (2 * N_ZC), gz),
        (gx, (gy + 2) % (2 * N_ZC), gz),
    ]
    barrier = pltpu.get_barrier_semaphore()
    greeted = [partner(delta)[0] for delta in range(1, 8)] + neighbours
    greeted += [along(steps) for steps in (1, 2, -1, -2)]
    for device in greeted:
        pl.semaphore_signal(barrier, inc=1, device_id=device, device_id_type=MESH)

    floor[...] = jnp.zeros_like(floor)
    update[...] = jnp.zeros_like(update)
    face_out[...] = jnp.zeros_like(face_out)
    sub = lax.broadcasted_iota(jnp.int32, (8, 128), 0)
    lane = lax.broadcasted_iota(jnp.int32, (8, 128), 1)
    bits = [jnp.where((lane & (1 << bit)) != 0, 1.0, 0.0) for bit in range(7)]
    k_mask = jnp.where(sub < 5, 1.0, 0.0)
    for node in range(5):
        column = jnp.zeros((8, 128), jnp.float32)
        for row in range(5):
            if TABLE[row, node] != 0.0:
                column = jnp.where(sub == row, float(TABLE[row, node]), column)
        coef[COL_D + node] = column

    lane1 = lax.broadcasted_iota(jnp.int32, (1, 128), 1)
    high1 = (lane1 & 64) != 0
    low1 = (lane1 & 32) != 0

    def element_row(ref):
        return jnp.where(
            high1,
            jnp.where(low1, ref[1, 0, 1], ref[1, 0, 0]),
            jnp.where(low1, ref[0, 0, 1], ref[0, 0, 0]),
        )

    def column_row(ref):
        return jnp.where(high1, ref[1, 0].astype(jnp.float32), ref[0, 0].astype(jnp.float32))

    load.wait()
    fields = swap_bits([staged[e // 2, 0, e % 2] for e in range(4)], FIELD_BITS)
    for field in range(4):
        nat[field, 0:125] = fields[field]
    nat[0, 125:126] = element_row(bulk)
    nat[0, 126:127] = element_row(buoy)
    nat[0, 127:128] = column_row(layers)
    cell_row = column_row(cells)
    nat[1, 125:126] = cell_row
    nat[1, 126:127] = cell_row
    nat[1, 127:128] = cell_row
    for field in (2, 3):
        nat[field, 125:128] = jnp.zeros((3, 128), jnp.float32)
    blocks = swap_bits([nat[:, 16 * at : 16 * at + 16, :] for at in range(8)], RANK_BITS)
    for at in range(8):
        pack_out[at] = blocks[at]

    pl.semaphore_wait(barrier, len(greeted))

    def swap_copy(out_ref, in_ref, send, recv, delta, by_owner=False):
        device, rank, to_y = partner(delta)
        return pltpu.make_async_remote_copy(
            src_ref=out_ref.at[to_y if by_owner else rank],
            dst_ref=in_ref.at[me],
            send_sem=send.at[delta],
            recv_sem=recv.at[delta],
            device_id=device,
            device_id_type=MESH,
        )

    order = (2, 3, 4, 5, 6, 7, 1)
    sends = [swap_copy(pack_out, pack_in, a_send, a_recv, delta) for delta in order]
    for copy in sends:
        copy.start()
    pack_in[me] = pack_out[me]
    for copy in sends:
        copy.wait_recv()

    blocks = swap_bits([pack_in[at] for at in range(8)], RANK_BITS)
    for at in range(8):
        nat[:, 16 * at : 16 * at + 16, :] = blocks[at]

    def wide(row):
        return jnp.broadcast_to(row, (8, 128))

    bulk_l = wide(nat[0, 125:126])
    buoy_l = wide(nat[0, 126:127])
    layers_l = wide(nat[0, 127:128])
    depth = 4.0 * bits[3] + 2.0 * bits[2] + bits[5]
    active = jnp.where(depth < layers_l, 1.0, 0.0)
    coef[SELECT] = jnp.where(depth == layers_l - 1.0, 1.0, 0.0)
    act_k = active * k_mask
    coef[ACTIVE] = act_k

    for line in range(25):
        state[0, :, 8 * line : 8 * line + 8, :] = nat[:, 5 * line : 5 * line + 8, :] * act_k

    def face_rows(ref, field, axis, side):
        node = 4 * side
        if axis == 0:
            return ref[field, 40 * node : 40 * node + 40, :].reshape(5, 8, 128)
        return jnp.stack([ref[field, 40 * i + 8 * node : 40 * i + 8 * node + 8, :] for i in range(5)])

    def face_copy(section, direction):
        return pltpu.make_async_remote_copy(
            src_ref=face_out.at[section, direction],
            dst_ref=face_in.at[section, direction],
            send_sem=h_send.at[section, direction],
            recv_sem=h_recv.at[section, direction],
            device_id=neighbours[direction + 1 - 2 * (direction % 2)],
            device_id_type=MESH,
        )

    def pack_two(first, second, direction):
        axis, side, bit, shift = face_of(direction)
        mask = bit_mask(first.shape, bit)
        moved = lane_roll(first, shift)
        return jnp.where(mask, moved, second) if side == 1 else jnp.where(mask, second, moved)

    def send_faces(section, ref, first):
        for direction in (2, 3, 0, 1):
            axis, side, bit, shift = face_of(direction)
            others = [1, 2, 3]
            others.remove(1 + axis)
            for half, (one, two) in enumerate(((0, 1 + axis), (others[0], others[1]))):
                packed = pack_two(
                    face_rows(ref, one, axis, 1 - side), face_rows(ref, two, axis, 1 - side), direction
                )
                for line in range(5):
                    at = 25 * half + 5 * line
                    face_out[section, direction, at : at + 8, :] = packed[line]
            if first:
                face_out[section, direction, 48:56, :] = jnp.where(
                    sub >= 5, pack_two(bulk_l, buoy_l, direction),
                    face_out[section, direction, 48:56, :],
                )
            face_copy(section, direction).start()

    send_faces(0, state.at[0], True)

    speed_l = jnp.sqrt(bulk_l * buoy_l)
    coef[BULK] = bulk_l
    coef[BUOY] = buoy_l
    coef[SPEED] = speed_l
    coef[VOL_B] = buoy_l * act_k
    coef[VOL_K] = bulk_l * act_k
    coef[VOL_G] = GRAVITY / buoy_l * act_k
    for direction in range(4):
        axis, side, bit, _ = face_of(direction)
        width = 1 << bit
        shift = width if side == 0 else -width
        mask = bits[bit] if side == 0 else 1.0 - bits[bit]
        use = 5.0 * act_k * mask
        sign = 1.0 if side == 1 else -1.0
        at = INNER + 3 * direction
        coef[at] = use * jnp.maximum(speed_l, lane_roll(speed_l, shift))
        coef[at + 1] = sign * use * lane_roll(buoy_l, shift)
        coef[at + 2] = sign * use * lane_roll(bulk_l, shift)

    def deeper(value, side):
        mask = bit_mask(value.shape, 5)
        if side == 0:
            return jnp.where(mask, lane_roll(value, 32), lane_roll(value, -28))
        return jnp.where(mask, lane_roll(value, 28), lane_roll(value, -32))

    for side in range(2):
        inside = jnp.where(depth > 0.5, 1.0, 0.0) if side == 0 else jnp.where(depth < 6.5, 1.0, 0.0)
        sign = 1.0 if side == 1 else -1.0
        jump = 5.0 * active * jnp.maximum(speed_l, inside * deeper(speed_l, side))
        at = Z_ROWS + 4 * side
        coef[at] = jump
        coef[at + 1] = jump * inside
        coef[at + 2] = sign * 5.0 * active * inside * deeper(buoy_l, side)
        coef[at + 3] = sign * 5.0 * active * inside * deeper(bulk_l, side)

    def row(index):
        return coef[index, 0:1, :]

    def trace_copy(steps):
        return pltpu.make_async_remote_copy(
            src_ref=tr_out,
            dst_ref=tr_in.at[steps - 1],
            send_sem=t_send.at[steps - 1],
            recv_sem=t_recv.at[steps - 1],
            device_id=along(steps),
            device_id_type=MESH,
        )

    def section(number, carry):
        now = lax.rem(number, 2)
        later = 1 - now
        stage = lax.rem(number, 4)
        ends = (stage == 0) | (stage == 3)
        share = jnp.where(ends, DT / 6.0, DT / 3.0).astype(jnp.float32)
        reach = jnp.where(stage == 3, DT / 6.0, jnp.where(stage == 2, DT, DT / 2.0)).astype(jnp.float32)
        keep = jnp.where(stage == 0, 0.0, 1.0).astype(jnp.float32)
        last = jnp.where(stage == 3, 1.0, 0.0).astype(jnp.float32)
        here, there = state.at[now], state.at[later]

        @pl.when(stage == 0)
        def _():
            base[...] = here[...]

        top = [here[field, pl.ds(0, 25, stride=8), :] for field in range(4)]
        bottom = [here[field, pl.ds(4, 25, stride=8), :] for field in range(4)]
        for field in range(4):
            floor[field] += share * bottom[field]

        @pl.when(number == SECTIONS - 1)
        def _():
            chosen = [floor[field] * row(SELECT) for field in range(4)]
            together = fold_bits(chosen, (2, 3))
            together = together + flip(together, 5)
            tr_out[0:25] = together
            tr_out[25:26] = nat[1, 125:126]
            tr_out[26:32] = jnp.zeros((6, 128), jnp.float32)
            from_lane = lax.broadcasted_iota(jnp.int32, (128, 128), 0)
            to_lane = lax.broadcasted_iota(jnp.int32, (128, 128), 1)
            wanted = jnp.zeros((128, 128), jnp.int32)
            for to_bit, from_bit in ((6, 3), (5, 2), (3, 6), (2, 4), (1, 1), (0, 0)):
                wanted = wanted + jnp.where((to_lane & (1 << to_bit)) != 0, 1 << from_bit, 0)
            table = jnp.where((from_lane == wanted) & ((to_lane & 16) == 0), 1.0, 0.0)
            tr_out[...] = jnp.dot(
                tr_out[...], table, precision=lax.Precision.HIGHEST,
                preferred_element_type=jnp.float32,
            )
            for steps in (1, 2):
                trace_copy(steps).start()

        def cube(field):
            return here[field].reshape(5, 5, 8, 128)

        def along_i(value):
            return jnp.stack([weighted(TABLE[i], [value[m] for m in range(5)]) for i in range(5)])

        def along_j(value):
            return jnp.stack(
                [weighted(TABLE[j], [value[:, m] for m in range(5)]) for j in range(5)], axis=1
            )

        def along_k(value):
            total = None
            for node in range(5):
                one = jnp.broadcast_to(value[:, :, node : node + 1, :], (5, 5, 8, 128))
                term = coef[COL_D + node] * one
                total = term if total is None else total + term
            return total

        def put(field, value):
            rate[field] = value.reshape(200, 128)

        pressure = cube(0)
        put(1, coef[VOL_K] * along_i(pressure))
        put(2, coef[VOL_K] * along_j(pressure))
        put(3, coef[VOL_K] * along_k(pressure) + coef[VOL_G] * pressure)
        put(0, coef[VOL_B] * (along_i(cube(1)) + along_j(cube(2)) + along_k(cube(3))))

        for direction in range(4):
            axis, side, bit, _ = face_of(direction)
            width = 1 << bit
            shift = width if side == 0 else -width
            at = INNER + 3 * direction
            outer = [lane_roll(face_rows(here, field, axis, 1 - side), shift) for field in range(4)]
            for field in range(4):
                add = coef[at] * (outer[field] - face_rows(here, field, axis, side))
                if field == 0:
                    add = add + coef[at + 1] * outer[1 + axis]
                if field == 1 + axis:
                    add = add + coef[at + 2] * outer[0]
                add_face(rate, field, axis, side, add, None)
        for side in range(2):
            at = Z_ROWS + 4 * side
            own = bottom if side == 1 else top
            outer = [deeper((top if side == 1 else bottom)[field], side) for field in range(4)]
            for field in range(4):
                add = row(at + 1) * outer[field] - row(at) * own[field]
                if field == 0:
                    add = add + row(at + 2) * outer[3]
                if field == 3:
                    add = add + row(at + 3) * outer[0]
                where = pl.ds(4 * side, 25, stride=8)
                rate[field, where, :] = rate[field, where, :] + add

        for field in range(4):
            now_rate = rate[field]
            before = update[field]
            there[field] = base[field] + (reach * now_rate + last * before)
            update[field] = keep * before + share * now_rate

        for direction in (2, 3, 0, 1):
            face_copy(number, direction).wait_recv()

        @pl.when(number == 0)
        def _():
            for direction in range(4):
                axis, side, bit, shift = face_of(direction)
                packed = jnp.broadcast_to(face_in[0, direction, 53:54, :], (8, 128))
                bulk_o, buoy_o = packed, lane_roll(packed, shift)
                if axis == 0:
                    limit = gx == (N_GX - 1 if side == 1 else 0)
                else:
                    limit = zc == (N_ZC - 1 if side == 1 else 0)
                inside = jnp.where(limit, 0.0, 1.0).astype(jnp.float32)
                mask = bits[bit] if side == 1 else 1.0 - bits[bit]
                use = 5.0 * coef[ACTIVE] * mask
                sign = 1.0 if side == 1 else -1.0
                jump = use * jnp.maximum(coef[SPEED], inside * jnp.sqrt(bulk_o * buoy_o))
                at = OUTER + 4 * direction
                coef[at] = jump
                coef[at + 1] = jump * inside
                coef[at + 2] = sign * inside * use * buoy_o
                coef[at + 3] = sign * inside * use * bulk_o

        for direction in range(4):
            axis, side, bit, shift = face_of(direction)
            others = [1, 2, 3]
            others.remove(1 + axis)
            at = OUTER + 4 * direction
            arrived = []
            for half in range(2):
                packed = jnp.stack(
                    [
                        face_in[number, direction, 25 * half + 5 * line : 25 * half + 5 * line + 8, :]
                        for line in range(5)
                    ]
                )
                arrived += [packed, lane_roll(packed, shift)]
            by_field = {0: arrived[0], 1 + axis: arrived[1], others[0]: arrived[2], others[1]: arrived[3]}
            for field in range(4):
                add = coef[at + 1] * by_field[field] - coef[at] * face_rows(here, field, axis, side)
                if field == 0:
                    add = add + coef[at + 2] * by_field[1 + axis]
                if field == 1 + axis:
                    add = add + coef[at + 3] * by_field[0]
                add_face(there, field, axis, side, add, reach)
                add_face(update, field, axis, side, add, share)

        @pl.when(number < SECTIONS - 1)
        def _():
            send_faces(number + 1, there, False)

        return carry

    def add_face(ref, field, axis, side, add, scale):
        node = 4 * side
        if scale is not None:
            add = scale * add
        if axis == 0:
            rows = slice(40 * node, 40 * node + 40)
            ref[field, rows, :] = ref[field, rows, :] + add.reshape(40, 128)
        else:
            for i in range(5):
                rows = slice(40 * i + 8 * node, 40 * i + 8 * node + 8)
                ref[field, rows, :] = ref[field, rows, :] + add[i]

    lax.fori_loop(0, SECTIONS, section, 0)

    for line in range(25):
        nat[:, 5 * line : 5 * line + 8, :] = state[0, :, 8 * line : 8 * line + 8, :]
    blocks = swap_bits([nat[:, 16 * at : 16 * at + 16, :] for at in range(8)], RANK_BITS)
    for at in range(8):
        back_out[at] = blocks[at]
    backs = [swap_copy(back_out, back_in, b_send, b_recv, delta) for delta in order]
    for copy in backs:
        copy.start()
    back_in[me] = back_out[me]

    for steps in (1, 2):
        trace_copy(steps).wait_recv()
    first_cell = ((gx * N_ZC + zc) * (2 * S_DEV)).astype(jnp.float32)
    sources = [tr_out, tr_in.at[0], tr_in.at[1]]
    values = [source[0:25] for source in sources]
    labels = [source[25:26] - first_cell for source in sources]
    for owner in range(2):
        picked = []
        for cell in range(S_DEV):
            total = None
            for value, label in zip(values, labels):
                hit = jnp.where(label == float(owner * S_DEV + cell), 1.0, 0.0)
                term = hit * value
                total = term if total is None else total + term
            picked.append(total)
        tb_out[owner] = fold_bits(picked, (2, 3, 4))
    ends = [swap_copy(tb_out, tb_in, c_send, c_recv, delta, True) for delta in order]
    for copy in ends:
        copy.start()
    tb_in[me] = tb_out[y_lo]

    for copy in backs:
        copy.wait_recv()
    blocks = swap_bits([back_in[at] for at in range(8)], RANK_BITS)
    for at in range(8):
        nat[:, 16 * at : 16 * at + 16, :] = blocks[at]
    elements = swap_bits([nat[field, 0:125] for field in range(4)], FIELD_BITS)
    for e in range(4):
        staged[e // 2, 0, e % 2] = elements[e]
    store = pltpu.make_async_copy(staged, out_hbm, local_sem.at[1])
    store.start()

    for copy in ends:
        copy.wait_recv()
    blocks = swap_bits([tb_in[at] for at in range(8)], RANK_BITS)
    for at in range(8):
        trace[at] = blocks[at]
    store_trace = pltpu.make_async_copy(trace, trace_hbm, local_sem.at[2])
    store_trace.start()

    for copy in sends + backs + ends:
        copy.wait_send()
    for steps in (1, 2):
        trace_copy(steps).wait_send()

    def drain(number, carry):
        for direction in range(4):
            face_copy(number, direction).wait_send()
        return carry

    lax.fori_loop(0, SECTIONS, drain, 0)
    store.wait()
    store_trace.wait()


def shards(adjoint_state, bulk_modulus, buoyancy, water_layers, surface_cell):
    f32 = jnp.float32
    in_smem = pl.BlockSpec(memory_space=pltpu.SMEM)
    in_any = pl.BlockSpec(memory_space=pl.ANY)
    dma = pltpu.SemaphoreType.DMA
    return pl.pallas_call(
        kernel,
        out_shape=(
            jax.ShapeDtypeStruct(adjoint_state.shape, f32),
            jax.ShapeDtypeStruct((S_DEV, 25, 128), f32),
        ),
        in_specs=[in_any, in_smem, in_smem, in_smem, in_smem],
        out_specs=(in_any, in_any),
        scratch_shapes=[
            pltpu.VMEM(adjoint_state.shape, f32),
            pltpu.VMEM((4, 128, 128), f32),
            pltpu.VMEM((8, 4, 16, 128), f32),
            pltpu.VMEM((8, 4, 16, 128), f32),
            pltpu.VMEM((8, 4, 16, 128), f32),
            pltpu.VMEM((8, 4, 16, 128), f32),
            pltpu.VMEM((2, 4, 200, 128), f32),
            pltpu.VMEM((4, 200, 128), f32),
            pltpu.VMEM((4, 200, 128), f32),
            pltpu.VMEM((4, 200, 128), f32),
            pltpu.VMEM((N_COEF, 8, 128), f32),
            pltpu.VMEM((SECTIONS, 4, 56, 128), f32),
            pltpu.VMEM((SECTIONS, 4, 56, 128), f32),
            pltpu.VMEM((4, 25, 128), f32),
            pltpu.VMEM((32, 128), f32),
            pltpu.VMEM((2, 32, 128), f32),
            pltpu.VMEM((2, 25, 128), f32),
            pltpu.VMEM((8, 25, 128), f32),
            pltpu.VMEM((8, 25, 128), f32),
            dma((3,)),
            dma((8,)),
            dma((8,)),
            dma((SECTIONS, 4)),
            dma((SECTIONS, 4)),
            dma((2,)),
            dma((2,)),
            dma((8,)),
            dma((8,)),
            dma((8,)),
            dma((8,)),
        ],
        compiler_params=pltpu.CompilerParams(
            collective_id=0, has_side_effects=True, vmem_limit_bytes=24 * 1024 * 1024
        ),
        name="adjoint_steps",
    )(adjoint_state, bulk_modulus, buoyancy, water_layers, surface_cell)


def solution(mesh):
    placed = (
        P("gx", "gy", "gz", None, None),
        P("gx", "gy", "gz"),
        P("gx", "gy", "gz"),
        P("gx", "gy"),
        P("gx", "gy"),
    )
    return jax.shard_map(
        shards,
        mesh=mesh,
        in_specs=placed,
        out_specs=(P("gx", "gy", "gz", None, None), P(("gx", "gy"), None, None)),
        check_vma=False,
    )
```

```python
import math

import jax
import jax.numpy as jnp
import numpy as np
from jax import lax
from jax.experimental import pallas as pl
from jax.experimental.pallas import tpu as pltpu
from jax.sharding import PartitionSpec as P

N_ZC = 8
RANKS = 32
STEPS = 2
S_DEV = 8
GRAVITY = 2.0
DT = 0.02
MESH = pl.DeviceIdType.MESH


def derivative_rows():
    points = np.array([-1.0, -math.sqrt(3.0 / 7.0), 0.0, math.sqrt(3.0 / 7.0), 1.0])
    scales = np.array(
        [np.prod([points[a] - points[b] for b in range(5) if b != a]) for a in range(5)]
    )
    table = np.zeros((5, 5))
    for a in range(5):
        for b in range(5):
            if a != b:
                table[a, b] = scales[a] / scales[b] / (points[a] - points[b])
        table[a, a] = -np.sum(table[a])
    table[0, 0] += 5.0
    table[4, 4] -= 5.0
    table[np.abs(table) < 1e-12] = 0.0
    return table


TABLE = derivative_rows()
KAPPA = float(np.dot(TABLE[0], TABLE[:, 0]))


def weighted(row, parts):
    total = None
    for weight, part in zip(row, parts):
        if weight != 0.0:
            term = float(weight) * part
            total = term if total is None else total + term
    return total


def bit_mask(shape, bit):
    lanes = lax.broadcasted_iota(jnp.int32, shape, len(shape) - 1)
    return (lanes & (1 << bit)) != 0


def lane_roll(value, shift):
    return pltpu.roll(value, shift % 128, axis=value.ndim - 1)


def swap_pair(low, high, bit):
    width = 1 << bit
    mask = bit_mask(low.shape, bit)
    return (
        jnp.where(mask, lane_roll(high, width), low),
        jnp.where(mask, high, lane_roll(low, -width)),
    )


def swap_stage(value, index_bit, lane_bit):
    step = 1 << index_bit
    shape = value.shape
    split = value.reshape((shape[0] // (2 * step), 2, step) + shape[1:])
    part = split[:, 0].shape
    flat = (-1,) + shape[-2:]
    low, high = swap_pair(split[:, 0].reshape(flat), split[:, 1].reshape(flat), lane_bit)
    return jnp.stack([low.reshape(part), high.reshape(part)], axis=1).reshape(shape)


def swap_bits(value, count):
    for bit in range(count):
        value = swap_stage(value, bit, bit)
    return value


def flip(value, bit):
    width = 1 << bit
    mask = bit_mask(value.shape, bit)
    return jnp.where(mask, lane_roll(value, width), lane_roll(value, -width))


def fold_pair(low, high, bit):
    mask = bit_mask(low.shape, bit)
    return jnp.where(mask, high, low) + flip(jnp.where(mask, low, high), bit)


def neighbour_lanes(value, axis, side):
    if axis == 1:
        return lane_roll(value, 1 if side == 0 else -1)
    wide, short, bit = (64, 56, 6) if axis == 0 else (32, 30, 5)
    mask = bit_mask(value.shape, bit)
    if side == 0:
        return jnp.where(mask, lane_roll(value, wide), lane_roll(value, -short))
    return jnp.where(mask, lane_roll(value, short), lane_roll(value, -wide))


VOL = 0
FACES = 3
SET = 19
GHOST = SET
INNER = 2 * SET
OUTER = INNER + 6
INTO = OUTER + 4
COL_D = INTO + 5
SELECT = COL_D + 5
BULK, BUOY, ACTIVE, SPEED = SELECT + 1, SELECT + 2, SELECT + 3, SELECT + 4
N_COEF = SPEED + 1


def kernel(
    state_hbm, bulk, buoy, layers, cells, out_hbm, trace_hbm,
    staged, nat, pack_out, pack_in, back_out, back_in, state, update, rate, coef,
    near, ghost, ghost_rate, face_out, face_in, floor, tr_out, tr_in, tb_out, tb_in, trace,
    local_sem, a_send, a_recv, h_send, h_recv, t_send, t_recv, b_send, b_recv, c_send, c_recv,
):
    gx = lax.axis_index("gx")
    gy = lax.axis_index("gy")
    gz = lax.axis_index("gz")
    zc, y_lo = gy // 2, gy % 2
    me = gx * 8 + gz * 2 + y_lo

    load = pltpu.make_async_copy(state_hbm, staged, local_sem.at[0])
    load.start()

    def device_of(rank):
        return (rank // 8, zc * 2 + rank % 2, (rank // 2) % 4)

    def layer(steps):
        return (gx, (gy + 2 * steps + 2 * N_ZC) % (2 * N_ZC), gz)

    barrier = pltpu.get_barrier_semaphore()

    def greet(delta, carry):
        pl.semaphore_signal(
            barrier, inc=1, device_id=device_of((me + delta) % RANKS), device_id_type=MESH
        )
        return carry

    lax.fori_loop(1, RANKS, greet, 0)
    for steps in (1, -1, 2, -2):
        pl.semaphore_signal(barrier, inc=1, device_id=layer(steps), device_id_type=MESH)

    floor[...] = jnp.zeros_like(floor)
    face_out[...] = jnp.zeros_like(face_out)
    sub = lax.broadcasted_iota(jnp.int32, (8, 128), 0)
    lane = lax.broadcasted_iota(jnp.int32, (8, 128), 1)
    bits = [jnp.where((lane & (1 << bit)) != 0, 1.0, 0.0) for bit in range(7)]
    k_mask = jnp.where(sub < 5, 1.0, 0.0)
    for node in range(5):
        column = jnp.zeros((8, 128), jnp.float32)
        for row_at in range(5):
            if TABLE[row_at, node] != 0.0:
                column = jnp.where(sub == row_at, float(TABLE[row_at, node]), column)
        coef[COL_D + node] = column

    lane1 = lax.broadcasted_iota(jnp.int32, (1, 128), 1)
    high1 = (lane1 & 64) != 0
    low1 = (lane1 & 32) != 0

    def element_row(ref):
        return jnp.where(
            high1,
            jnp.where(low1, ref[1, 0, 1], ref[1, 0, 0]),
            jnp.where(low1, ref[0, 0, 1], ref[0, 0, 0]),
        )

    def column_row(ref):
        return jnp.where(high1, ref[0, 1].astype(jnp.float32), ref[0, 0].astype(jnp.float32))

    def blocks_of(ref):
        return jnp.stack(
            [
                jnp.stack([ref[low, 8 * tile : 8 * tile + 8], ref[2 + low, 8 * tile : 8 * tile + 8]])
                for tile in range(16)
                for low in range(2)
            ]
        )

    def put_blocks(ref, value):
        for at in range(32):
            tile, low = at // 2, at % 2
            for high in range(2):
                ref[2 * high + low, 8 * tile : 8 * tile + 8] = value[at, high]

    def field_swap(parts):
        for step, bit in ((1, 5), (2, 6)):
            for at in range(4):
                if not at & step:
                    parts[at], parts[at + step] = swap_pair(parts[at], parts[at + step], bit)
        return parts

    load.wait()
    fields = field_swap([staged[e // 2, 0, :, e % 2, :] for e in range(4)])
    for field in range(4):
        nat[field, 0:125] = fields[field]
    nat[0, 125:126] = element_row(bulk)
    nat[0, 126:127] = element_row(buoy)
    nat[0, 127:128] = column_row(layers)
    cell_row = column_row(cells)
    nat[1, 125:126] = cell_row
    nat[1, 126:127] = cell_row
    nat[1, 127:128] = cell_row
    for field in (2, 3):
        nat[field, 125:128] = jnp.zeros((3, 128), jnp.float32)
    pack_out[...] = swap_bits(blocks_of(nat), 5).reshape(32, 16, 128)

    pl.semaphore_wait(barrier, RANKS - 1 + 4)

    def swap_copy(out_ref, in_ref, send, recv, delta, by_owner):
        rank = (me + delta) % RANKS
        return pltpu.make_async_remote_copy(
            src_ref=out_ref.at[(rank // 8) * 2 + rank % 2 if by_owner else rank],
            dst_ref=in_ref.at[me],
            send_sem=send.at[delta],
            recv_sem=recv.at[delta],
            device_id=device_of(rank),
            device_id_type=MESH,
        )

    def each(work, out_ref, in_ref, send, recv, by_owner=False):
        def one(delta, carry):
            work(swap_copy(out_ref, in_ref, send, recv, delta, by_owner))
            return carry

        lax.fori_loop(1, RANKS, one, 0)

    def start(copy):
        copy.start()

    def arrive(copy):
        copy.wait_recv()

    def leave(copy):
        copy.wait_send()

    into = (pack_out, pack_in, a_send, a_recv)
    each(start, *into)
    pack_in[me] = pack_out[me]
    each(arrive, *into)
    put_blocks(nat, swap_bits(pack_in[...].reshape(32, 2, 8, 128), 5))

    def wide(row_value):
        return jnp.broadcast_to(row_value, (8, 128))

    bulk_l = wide(nat[0, 125:126])
    buoy_l = wide(nat[0, 126:127])
    layers_l = wide(nat[0, 127:128])
    depth = 4.0 * bits[2] + 2.0 * bits[1] + bits[5]
    strike = 4.0 * bits[4] + 2.0 * bits[3] + bits[6]
    active = jnp.where(depth < layers_l, 1.0, 0.0)
    act_k = active * k_mask

    for line in range(25):
        state[0, :, 8 * line : 8 * line + 8, :] = nat[:, 5 * line : 5 * line + 8, :] * act_k

    def face_rows(ref, field, axis, side):
        node = 4 * side
        if axis == 0:
            return ref[field, 40 * node : 40 * node + 40, :].reshape(5, 8, 128)
        return jnp.stack([ref[field, 40 * i + 8 * node : 40 * i + 8 * node + 8, :] for i in range(5)])

    def face_copy(step, number, direction):
        return pltpu.make_async_remote_copy(
            src_ref=face_out.at[step, number, direction],
            dst_ref=face_in.at[step, number, direction],
            send_sem=h_send.at[step, number, direction],
            recv_sem=h_recv.at[step, number, direction],
            device_id=layer(1 - 2 * direction),
            device_id_type=MESH,
        )

    def pack_two(first, second, direction):
        mask = bit_mask(first.shape, 0)
        if direction == 0:
            return jnp.where(mask, second, lane_roll(first, -1))
        return jnp.where(mask, lane_roll(first, 1), second)

    def near_planes(ref):
        out = []
        for field in range(4):
            low, high = face_rows(ref, field, 1, 0), face_rows(ref, field, 1, 1)
            out.append(jnp.where(bit_mask(low.shape, 0), high, low))
        return out

    def send_planes(step, number, planes):
        for direction in range(2):
            for half, (one, two) in enumerate(((0, 2), (1, 3))):
                packed = pack_two(planes[one], planes[two], direction)
                for line in range(5):
                    at = 25 * half + 5 * line
                    face_out[step, number, direction, at : at + 8, :] = packed[line]
            if number == 0:
                extra = jnp.where(
                    sub == 5,
                    pack_two(coef[BULK], coef[BUOY], direction),
                    pack_two(coef[ACTIVE], coef[ACTIVE], direction),
                )
                face_out[step, number, direction, 48:56, :] = jnp.where(
                    sub >= 5, extra, face_out[step, number, direction, 48:56, :]
                )
            face_copy(step, number, direction).start()

    def unpack_two(below, above):
        mask = bit_mask(below.shape, 0)
        return jnp.where(mask, above, below), flip(jnp.where(mask, below, above), 0)

    def arrived_planes(step, number):
        for direction in range(2):
            face_copy(step, number, direction).wait_recv()
        out = []
        for half in range(2):
            rows = [
                jnp.stack(
                    [
                        face_in[step, number, direction, 25 * half + 5 * line : 25 * half + 5 * line + 8, :]
                        for line in range(5)
                    ]
                )
                for direction in range(2)
            ]
            out.append(unpack_two(rows[0], rows[1]))
        return [out[0][0], out[1][0], out[0][1], out[1][1]]

    coef[BULK] = bulk_l
    coef[BUOY] = buoy_l
    coef[ACTIVE] = active
    send_planes(0, 0, near_planes(state.at[0]))

    def element_coefs(at, bulk_e, buoy_e, active_e):
        speed_e = jnp.sqrt(bulk_e * buoy_e)
        use = active_e * k_mask
        coef[at + VOL] = buoy_e * use
        coef[at + VOL + 1] = bulk_e * use
        coef[at + VOL + 2] = GRAVITY / buoy_e * use
        for number, (axis, place) in enumerate(((0, strike), (2, depth))):
            for side in range(2):
                inside = jnp.where(place > 0.5, 1.0, 0.0) if side == 0 else jnp.where(place < 6.5, 1.0, 0.0)
                sign = 1.0 if side == 1 else -1.0
                scale = 5.0 * (use if axis == 0 else active_e)
                jump = scale * jnp.maximum(speed_e, inside * neighbour_lanes(speed_e, axis, side))
                to = at + FACES + 8 * number + 4 * side
                coef[to] = jump
                coef[to + 1] = jump * inside
                coef[to + 2] = sign * scale * inside * neighbour_lanes(buoy_e, axis, side)
                coef[to + 3] = sign * scale * inside * neighbour_lanes(bulk_e, axis, side)
        return speed_e

    speed_l = element_coefs(0, bulk_l, buoy_l, active)
    coef[SPEED] = speed_l
    coef[SELECT] = jnp.where(depth == layers_l - 1.0, 1.0, 0.0)
    for side in range(2):
        use = 5.0 * act_k * (bits[0] if side == 0 else 1.0 - bits[0])
        sign = 1.0 if side == 1 else -1.0
        at = INNER + 3 * side
        coef[at] = use * jnp.maximum(speed_l, neighbour_lanes(speed_l, 1, side))
        coef[at + 1] = sign * use * neighbour_lanes(buoy_l, 1, side)
        coef[at + 2] = sign * use * neighbour_lanes(bulk_l, 1, side)

    def outer_coefs():
        packed = [
            [jnp.broadcast_to(face_in[0, 0, direction, at : at + 1, :], (8, 128)) for direction in range(2)]
            for at in (53, 54)
        ]
        bulk_o, buoy_o = unpack_two(packed[0][0], packed[0][1])
        active_o = unpack_two(packed[1][0], packed[1][1])[0]
        speed_o = element_coefs(GHOST, bulk_o, buoy_o, active_o)
        has_low = jnp.where(zc == 0, 0.0, 1.0).astype(jnp.float32)
        has_high = jnp.where(zc == N_ZC - 1, 0.0, 1.0).astype(jnp.float32)
        inside = has_low * (1.0 - bits[0]) + has_high * bits[0]
        sign = 2.0 * bits[0] - 1.0
        speed = jnp.maximum(coef[SPEED], inside * speed_o)
        use = 5.0 * coef[ACTIVE] * k_mask
        coef[OUTER] = use * speed
        coef[OUTER + 1] = use * speed * inside
        coef[OUTER + 2] = use * sign * inside * buoy_o
        coef[OUTER + 3] = use * sign * inside * bulk_o
        use_o = 5.0 * active_o * k_mask * inside
        coef[INTO] = use_o * speed
        coef[INTO + 1] = use_o * speed
        coef[INTO + 2] = -sign * use_o * coef[BUOY]
        coef[INTO + 3] = -sign * use_o * coef[BULK]
        coef[INTO + 4] = KAPPA * bulk_o * buoy_o * active_o * k_mask

    def row(index):
        return coef[index, 0:1, :]

    def rates(src, dst, planes, base):
        def cube(field):
            return src[field].reshape(5, planes, 8, 128)

        def along_i(value):
            return jnp.stack([weighted(TABLE[i], [value[m] for m in range(5)]) for i in range(5)])

        def along_j(value):
            return jnp.stack(
                [weighted(TABLE[j], [value[:, m] for m in range(5)]) for j in range(5)], axis=1
            )

        def along_k(value):
            total = None
            for node in range(5):
                one = jnp.broadcast_to(value[:, :, node : node + 1, :], value.shape)
                term = coef[COL_D + node] * one
                total = term if total is None else total + term
            return total

        def put(field, value):
            dst[field] = value.reshape(40 * planes, 128)

        vol_b, vol_k, vol_g = coef[base + VOL], coef[base + VOL + 1], coef[base + VOL + 2]
        pressure = cube(0)
        put(1, vol_k * along_i(pressure))
        put(2, vol_k * along_j(pressure) if planes == 5 else jnp.zeros_like(pressure))
        put(3, vol_k * along_k(pressure) + vol_g * pressure)
        total = along_i(cube(1)) + along_k(cube(3))
        if planes == 5:
            total = total + along_j(cube(2))
        put(0, vol_b * total)

        size = 8 * planes

        def x_face(ref, field, side):
            return ref[field, 4 * size * side : 4 * size * side + size, :].reshape(planes, 8, 128)

        for side in range(2):
            at = base + FACES + 4 * side
            outer = [neighbour_lanes(x_face(src, field, 1 - side), 0, side) for field in range(4)]
            for field in range(4):
                add = coef[at + 1] * outer[field] - coef[at] * x_face(src, field, side)
                if field == 0:
                    add = add + coef[at + 2] * outer[1]
                if field == 1:
                    add = add + coef[at + 3] * outer[0]
                rows = slice(4 * size * side, 4 * size * side + size)
                dst[field, rows, :] = dst[field, rows, :] + add.reshape(size, 128)

        if planes == 5:
            for side in range(2):
                at = INNER + 3 * side
                outer = [neighbour_lanes(face_rows(src, field, 1, 1 - side), 1, side) for field in range(4)]
                for field in range(4):
                    add = coef[at] * (outer[field] - face_rows(src, field, 1, side))
                    if field == 0:
                        add = add + coef[at + 1] * outer[2]
                    if field == 2:
                        add = add + coef[at + 2] * outer[0]
                    for i in range(5):
                        rows = slice(40 * i + 32 * side, 40 * i + 32 * side + 8)
                        dst[field, rows, :] = dst[field, rows, :] + add[i]

        lines = [[src[field, pl.ds(4 * side, 5 * planes, stride=8), :] for field in range(4)] for side in range(2)]
        for side in range(2):
            at = base + FACES + 8 + 4 * side
            outer = [neighbour_lanes(lines[1 - side][field], 2, side) for field in range(4)]
            for field in range(4):
                add = row(at + 1) * outer[field] - row(at) * lines[side][field]
                if field == 0:
                    add = add + row(at + 2) * outer[3]
                if field == 3:
                    add = add + row(at + 3) * outer[0]
                where = pl.ds(4 * side, 5 * planes, stride=8)
                dst[field, where, :] = dst[field, where, :] + add

    def flux(at, other, own):
        out = [coef[at + 1] * other[field] - coef[at] * own[field] for field in range(4)]
        out[0] = out[0] + coef[at + 2] * other[2]
        out[2] = out[2] + coef[at + 3] * other[0]
        return out

    def add_outer(ref, adds, scale):
        for field in range(4):
            add = scale * adds[field]
            mask = bit_mask(add.shape, 0)
            low, high = jnp.where(mask, 0.0, add), jnp.where(mask, add, 0.0)
            for i in range(5):
                for part, at in ((low, 40 * i), (high, 40 * i + 32)):
                    ref[field, at : at + 8, :] = ref[field, at : at + 8, :] + part[i]

    def add_floor(ref, share):
        for field in range(4):
            floor[field] += share * ref[field, pl.ds(4, 25, stride=8), :]

    def trace_copy(steps):
        return pltpu.make_async_remote_copy(
            src_ref=tr_out,
            dst_ref=tr_in.at[steps - 1],
            send_sem=t_send.at[steps - 1],
            recv_sem=t_recv.at[steps - 1],
            device_id=layer(steps),
            device_id_type=MESH,
        )

    def send_floor():
        chosen = [floor[field] * row(SELECT) for field in range(4)]
        pair = [fold_pair(chosen[0], chosen[1], 1), fold_pair(chosen[2], chosen[3], 1)]
        together = fold_pair(pair[0], pair[1], 2)
        tr_out[0:25] = together + flip(together, 5)
        tr_out[25:26] = nat[1, 125:126]
        tr_out[26:32] = jnp.zeros((6, 128), jnp.float32)
        for steps in (1, 2):
            trace_copy(steps).start()

    def as_planes(ref):
        return [ref[field].reshape(5, 8, 128) for field in range(4)]

    def put_planes(ref, planes):
        for field in range(4):
            ref[field] = planes[field].reshape(40, 128)

    half, sixth, third = DT / 2.0, DT / 6.0, DT / 3.0
    now, first, second, third_in = state.at[0], state.at[1], state.at[2], state.at[3]

    def time_step(step, carry):
        add_floor(now, sixth)
        rates(now, rate, 5, 0)
        for field in range(4):
            first[field] = now[field] + half * rate[field]
            update[field] = sixth * rate[field]
        send_planes(step, 1, near_planes(first))
        rates(first, rate, 5, 0)
        for field in range(4):
            second[field] = now[field] + half * rate[field]
        planes = near_planes(second)
        send_planes(step, 2, planes)
        put_planes(near, planes)
        rates(near, ghost_rate, 1, 0)

        def across(field):
            value = second[field].reshape(5, 5, 8, 128)
            parts = [value[:, m] for m in range(5)]
            low, high = weighted(TABLE[0], parts), weighted(TABLE[4], parts)
            return jnp.where(bit_mask(low.shape, 0), high, low)

        slopes = as_planes(ghost_rate)
        slopes[0] = slopes[0] + coef[VOL] * across(2)
        slopes[2] = slopes[2] + coef[VOL + 1] * across(0)
        starts = near_planes(now)
        send_planes(step, 3, [starts[field] + DT * slopes[field] for field in range(4)])

        outer = arrived_planes(step, 0)

        @pl.when(step == 0)
        def _():
            outer_coefs()

        own = near_planes(now)
        adds = flux(OUTER, outer, own)
        add_outer(first, adds, half)
        add_outer(update, adds, sixth)
        answer = [half * term for term in flux(INTO, own, outer)]
        put_planes(ghost.at[0], answer)
        free = arrived_planes(step, 1)
        outer = [free[field] + answer[field] for field in range(4)]

        add_floor(first, third)
        rates(first, rate, 5, 0)
        own = near_planes(first)
        adds = flux(OUTER, outer, own)
        for field in range(4):
            second[field] = now[field] + half * rate[field]
            update[field] = update[field] + third * rate[field]
        add_outer(second, adds, half)
        add_outer(update, adds, third)
        rates(ghost.at[0], ghost_rate, 1, GHOST)
        slopes = as_planes(ghost_rate)
        answer = [half * (slopes[field] + term) for field, term in enumerate(flux(INTO, own, outer))]
        put_planes(ghost.at[1], answer)
        free = arrived_planes(step, 2)
        outer = [free[field] + answer[field] for field in range(4)]

        add_floor(second, third)
        rates(second, rate, 5, 0)
        own = near_planes(second)
        adds = flux(OUTER, outer, own)
        for field in range(4):
            third_in[field] = now[field] + DT * rate[field]
            update[field] = update[field] + third * rate[field]
        add_outer(third_in, adds, DT)
        add_outer(update, adds, third)
        rates(ghost.at[1], ghost_rate, 1, GHOST)
        slopes = as_planes(ghost_rate)
        early = as_planes(ghost.at[0])
        for field in (0, 2):
            slopes[field] = slopes[field] + half * (coef[INTO + 4] * early[field])
        answer = [DT * (slopes[field] + term) for field, term in enumerate(flux(INTO, own, outer))]
        free = arrived_planes(step, 3)
        outer = [free[field] + answer[field] for field in range(4)]

        add_floor(third_in, sixth)

        @pl.when(step == STEPS - 1)
        def _():
            send_floor()

        rates(third_in, rate, 5, 0)
        adds = flux(OUTER, outer, near_planes(third_in))
        for field in range(4):
            now[field] = now[field] + update[field] + sixth * rate[field]
        add_outer(now, adds, sixth)

        @pl.when(step < STEPS - 1)
        def _():
            send_planes(step + 1, 0, near_planes(now))

        return carry

    lax.fori_loop(0, STEPS, time_step, 0)

    for line in range(25):
        nat[:, 5 * line : 5 * line + 8, :] = now[:, 8 * line : 8 * line + 8, :]
    back_out[...] = swap_bits(blocks_of(nat), 5).reshape(32, 16, 128)
    back = (back_out, back_in, b_send, b_recv)
    each(start, *back)
    back_in[me] = back_out[me]

    for steps in (1, 2):
        trace_copy(steps).wait_recv()
    from_lane = lax.broadcasted_iota(jnp.int32, (128, 128), 0)
    to_lane = lax.broadcasted_iota(jnp.int32, (128, 128), 1)
    same_field = ((from_lane // 2) % 4 == to_lane // 32) & ((from_lane // 32) % 2 == 0)
    sources = [tr_out, tr_in.at[0], tr_in.at[1]]
    labels = [
        jnp.transpose(jnp.broadcast_to(source[25:26], (128, 128))).astype(jnp.int32) for source in sources
    ]
    for upper in range(2):
        owner = (upper * 2 + (to_lane // 2) % 2) * (2 * N_ZC) + 2 * zc + to_lane % 2
        cell = owner * S_DEV + (to_lane // 4) % 8
        total = None
        for source, label in zip(sources, labels):
            chosen = jnp.where(same_field & (label == cell), 1.0, 0.0)
            term = jnp.dot(
                source[...], chosen, precision=lax.Precision.HIGHEST, preferred_element_type=jnp.float32
            )
            total = term if total is None else total + term
        tb_out[4 * upper : 4 * upper + 4] = swap_bits(total.reshape(4, 8, 128), 2)
    ends = (tb_out, tb_in, c_send, c_recv, True)
    each(start, *ends)
    tb_in[me] = tb_out[gx * 2 + y_lo]

    each(arrive, *back)
    put_blocks(nat, swap_bits(back_in[...].reshape(32, 2, 8, 128), 5))
    elements = field_swap([nat[field, 0:125] for field in range(4)])
    for e in range(4):
        staged[e // 2, 0, :, e % 2, :] = elements[e]
    store = pltpu.make_async_copy(staged, out_hbm, local_sem.at[1])
    store.start()

    each(arrive, *ends)
    sums = swap_bits(tb_in[...], 5).reshape(8, 32, 128)
    for cell in range(S_DEV):
        trace[pl.ds(cell, 25, stride=8), :] = sums[cell, 0:25]
    store_trace = pltpu.make_async_copy(trace, trace_hbm, local_sem.at[2])
    store_trace.start()

    each(leave, *into)
    each(leave, *back)
    each(leave, *ends)
    for steps in (1, 2):
        trace_copy(steps).wait_send()

    def drain(step, carry):
        for number in range(4):
            for direction in range(2):
                face_copy(step, number, direction).wait_send()
        return carry

    lax.fori_loop(0, STEPS, drain, 0)
    store.wait()
    store_trace.wait()


def shards(adjoint_state, bulk_modulus, buoyancy, water_layers, surface_cell):
    f32 = jnp.float32
    in_smem = pl.BlockSpec(memory_space=pltpu.SMEM)
    in_any = pl.BlockSpec(memory_space=pl.ANY)
    dma = pltpu.SemaphoreType.DMA
    by_node = jnp.transpose(adjoint_state, (0, 1, 3, 2, 4))
    out, trace = pl.pallas_call(
        kernel,
        out_shape=(
            jax.ShapeDtypeStruct(by_node.shape, f32),
            jax.ShapeDtypeStruct((S_DEV * 25, 128), f32),
        ),
        in_specs=[in_any, in_smem, in_smem, in_smem, in_smem],
        out_specs=(in_any, in_any),
        scratch_shapes=[
            pltpu.VMEM(by_node.shape, f32),
            pltpu.VMEM((4, 128, 128), f32),
            pltpu.VMEM((32, 16, 128), f32),
            pltpu.VMEM((32, 16, 128), f32),
            pltpu.VMEM((32, 16, 128), f32),
            pltpu.VMEM((32, 16, 128), f32),
            pltpu.VMEM((4, 4, 200, 128), f32),
            pltpu.VMEM((4, 200, 128), f32),
            pltpu.VMEM((4, 200, 128), f32),
            pltpu.VMEM((N_COEF, 8, 128), f32),
            pltpu.VMEM((4, 40, 128), f32),
            pltpu.VMEM((2, 4, 40, 128), f32),
            pltpu.VMEM((4, 40, 128), f32),
            pltpu.VMEM((STEPS, 4, 2, 56, 128), f32),
            pltpu.VMEM((STEPS, 4, 2, 56, 128), f32),
            pltpu.VMEM((4, 25, 128), f32),
            pltpu.VMEM((32, 128), f32),
            pltpu.VMEM((2, 32, 128), f32),
            pltpu.VMEM((8, 8, 128), f32),
            pltpu.VMEM((32, 8, 128), f32),
            pltpu.VMEM((S_DEV * 25, 128), f32),
            dma((3,)),
            dma((RANKS,)),
            dma((RANKS,)),
            dma((STEPS, 4, 2)),
            dma((STEPS, 4, 2)),
            dma((2,)),
            dma((2,)),
            dma((RANKS,)),
            dma((RANKS,)),
            dma((RANKS,)),
            dma((RANKS,)),
        ],
        compiler_params=pltpu.CompilerParams(
            collective_id=0, has_side_effects=True, vmem_limit_bytes=24 * 1024 * 1024
        ),
        name="adjoint_steps",
    )(by_node, bulk_modulus, buoyancy, water_layers.T, surface_cell.T)
    return (
        jnp.transpose(out, (0, 1, 3, 2, 4)),
        jnp.transpose(trace.reshape(25, S_DEV, 128), (1, 0, 2)),
    )


def solution(mesh):
    placed = (
        P("gx", "gy", "gz", None, None),
        P("gx", "gy", "gz"),
        P("gx", "gy", "gz"),
        P("gx", "gy"),
        P("gx", "gy"),
    )
    return jax.shard_map(
        shards,
        mesh=mesh,
        in_specs=placed,
        out_specs=(P("gx", "gy", "gz", None, None), P(("gx", "gy"), None, None)),
        check_vma=False,
    )
```

```python
import math

import jax
import jax.numpy as jnp
import numpy as np
from jax import lax
from jax.experimental import pallas as pl
from jax.experimental.pallas import tpu as pltpu
from jax.sharding import PartitionSpec as P

N_ZC = 8
RANKS = 32
STEPS = 2
S_DEV = 8
GRAVITY = 2.0
DT = 0.02
MESH = pl.DeviceIdType.MESH


def derivative_rows():
    points = np.array([-1.0, -math.sqrt(3.0 / 7.0), 0.0, math.sqrt(3.0 / 7.0), 1.0])
    scales = np.array(
        [np.prod([points[a] - points[b] for b in range(5) if b != a]) for a in range(5)]
    )
    table = np.zeros((5, 5))
    for a in range(5):
        for b in range(5):
            if a != b:
                table[a, b] = scales[a] / scales[b] / (points[a] - points[b])
        table[a, a] = -np.sum(table[a])
    table[0, 0] += 5.0
    table[4, 4] -= 5.0
    table[np.abs(table) < 1e-12] = 0.0
    return table


TABLE = derivative_rows()
KAPPA = float(np.dot(TABLE[0], TABLE[:, 0]))


def weighted(row, parts):
    total = None
    for weight, part in zip(row, parts):
        if weight != 0.0:
            term = float(weight) * part
            total = term if total is None else total + term
    return total


def bit_mask(shape, bit):
    lanes = lax.broadcasted_iota(jnp.int32, shape, len(shape) - 1)
    return (lanes & (1 << bit)) != 0


def lane_roll(value, shift):
    return pltpu.roll(value, shift % 128, axis=value.ndim - 1)


def swap_pair(low, high, bit):
    width = 1 << bit
    mask = bit_mask(low.shape, bit)
    return (
        jnp.where(mask, lane_roll(high, width), low),
        jnp.where(mask, high, lane_roll(low, -width)),
    )


def swap_stage(value, index_bit, lane_bit):
    step = 1 << index_bit
    shape = value.shape
    split = value.reshape((shape[0] // (2 * step), 2, step) + shape[1:])
    part = split[:, 0].shape
    flat = (-1,) + shape[-2:]
    low, high = swap_pair(split[:, 0].reshape(flat), split[:, 1].reshape(flat), lane_bit)
    return jnp.stack([low.reshape(part), high.reshape(part)], axis=1).reshape(shape)


def swap_bits(value, count):
    for bit in range(count):
        value = swap_stage(value, bit, bit)
    return value


def flip(value, bit):
    width = 1 << bit
    mask = bit_mask(value.shape, bit)
    return jnp.where(mask, lane_roll(value, width), lane_roll(value, -width))


def fold_pair(low, high, bit):
    mask = bit_mask(low.shape, bit)
    return jnp.where(mask, high, low) + flip(jnp.where(mask, low, high), bit)


def neighbour_lanes(value, axis, side):
    if axis == 1:
        return lane_roll(value, 1 if side == 0 else -1)
    wide, short, bit = (64, 56, 6) if axis == 0 else (32, 30, 5)
    mask = bit_mask(value.shape, bit)
    if side == 0:
        return jnp.where(mask, lane_roll(value, wide), lane_roll(value, -short))
    return jnp.where(mask, lane_roll(value, short), lane_roll(value, -wide))


VOL = 0
FACES = 3
SET = 19
GHOST = SET
INNER = 2 * SET
OUTER = INNER + 6
INTO = OUTER + 4
COL_D = INTO + 5
SELECT = COL_D + 5
BULK, BUOY, ACTIVE, SPEED = SELECT + 1, SELECT + 2, SELECT + 3, SELECT + 4
N_COEF = SPEED + 1


def kernel(
    state_hbm, bulk_hbm, buoy_hbm, layers_hbm, cells_hbm, out, trace,
    bulk, buoy, layers, cells,
    staged, nat, pack_out, pack_in, back_out, back_in, state, update, rate, coef,
    near, ghost, ghost_rate, face_out, face_in, floor, tr_out, tr_in, label_out, label_in, chosen, tb_out, tb_in,
    local_sem, a_send, a_recv, h_send, h_recv, t_send, t_recv, b_send, b_recv, c_send, c_recv,
):
    gx = lax.axis_index("gx")
    gy = lax.axis_index("gy")
    gz = lax.axis_index("gz")
    zc, y_lo = gy // 2, gy % 2
    me = gx * 8 + gz * 2 + y_lo

    load = pltpu.make_async_copy(state_hbm, staged, local_sem.at[0])
    load.start()
    small = [
        pltpu.make_async_copy(source, target, local_sem.at[1 + at])
        for at, (source, target) in enumerate(
            ((bulk_hbm, bulk), (buoy_hbm, buoy), (layers_hbm, layers), (cells_hbm, cells))
        )
    ]
    for copy in small:
        copy.start()

    def device_of(rank):
        return (rank // 8, zc * 2 + rank % 2, (rank // 2) % 4)

    def layer(steps):
        return (gx, (gy + 2 * steps + 2 * N_ZC) % (2 * N_ZC), gz)

    barrier = pltpu.get_barrier_semaphore()

    has_below, has_above = zc > 0, zc < N_ZC - 1

    def greet(device):
        pl.semaphore_signal(barrier, inc=1, device_id=device, device_id_type=MESH)

    for delta in range(1, RANKS):
        greet(device_of((me + delta) % RANKS))

    @pl.when(has_below)
    def _():
        greet(layer(-1))

    @pl.when(has_above)
    def _():
        greet(layer(1))

    @pl.when(zc == 0)
    def _():
        greet(layer(-1))
        greet(layer(-2))

    @pl.when(zc == 1)
    def _():
        greet(layer(-2))

    greetings = (
        RANKS - 1
        + has_below.astype(jnp.int32)
        + has_above.astype(jnp.int32)
        + (zc == N_ZC - 2).astype(jnp.int32)
        + 2 * (zc == N_ZC - 1).astype(jnp.int32)
    )

    floor[...] = jnp.zeros_like(floor)
    face_out[...] = jnp.zeros_like(face_out)

    @pl.when(zc == 0)
    def _():
        face_in[:, 0] = jnp.zeros((STEPS, 4, 56, 128), jnp.float32)

    @pl.when(zc == N_ZC - 1)
    def _():
        face_in[:, 1] = jnp.zeros((STEPS, 4, 56, 128), jnp.float32)

    sub = lax.broadcasted_iota(jnp.int32, (8, 128), 0)
    lane = lax.broadcasted_iota(jnp.int32, (8, 128), 1)
    bits = [jnp.where((lane & (1 << bit)) != 0, 1.0, 0.0) for bit in range(7)]
    k_mask = jnp.where(sub < 5, 1.0, 0.0)
    for node in range(5):
        column = jnp.zeros((8, 128), jnp.float32)
        for row_at in range(5):
            if TABLE[row_at, node] != 0.0:
                column = jnp.where(sub == row_at, float(TABLE[row_at, node]), column)
        coef[COL_D + node] = column

    lane1 = lax.broadcasted_iota(jnp.int32, (1, 128), 1)
    high1 = (lane1 & 64) != 0
    low1 = (lane1 & 32) != 0

    def element_row(ref):
        return jnp.where(
            high1,
            jnp.where(low1, ref[1, 0, 1], ref[1, 0, 0]),
            jnp.where(low1, ref[0, 0, 1], ref[0, 0, 0]),
        )

    def column_row(ref):
        return jnp.where(high1, ref[0, 1].astype(jnp.float32), ref[0, 0].astype(jnp.float32))

    def blocks_of(ref):
        return jnp.stack(
            [
                jnp.stack([ref[low, 8 * tile : 8 * tile + 8], ref[2 + low, 8 * tile : 8 * tile + 8]])
                for tile in range(16)
                for low in range(2)
            ]
        )

    def put_blocks(ref, value):
        for at in range(32):
            tile, low = at // 2, at % 2
            for high in range(2):
                ref[2 * high + low, 8 * tile : 8 * tile + 8] = value[at, high]

    def field_swap(parts):
        for step, bit in ((1, 5), (2, 6)):
            for at in range(4):
                if not at & step:
                    parts[at], parts[at + step] = swap_pair(parts[at], parts[at + step], bit)
        return parts

    load.wait()
    for copy in small:
        copy.wait()
    fields = field_swap([staged[e // 2, 0, :, e % 2, :] for e in range(4)])
    for field in range(4):
        nat[field, 0:125] = fields[field]
    nat[0, 125:126] = element_row(bulk)
    nat[0, 126:127] = element_row(buoy)
    nat[0, 127:128] = column_row(layers)
    cell_row = column_row(cells)
    nat[1, 125:126] = cell_row
    nat[1, 126:127] = cell_row
    nat[1, 127:128] = cell_row
    for field in (2, 3):
        nat[field, 125:128] = jnp.zeros((3, 128), jnp.float32)
    pack_out[...] = swap_bits(blocks_of(nat), 5).reshape(32, 16, 128)

    pl.semaphore_wait(barrier, greetings)

    def start(copy):
        copy.start()

    def leave(copy):
        copy.wait_send()

    def swap_start(out_ref, in_ref, send, recv, by_owner=False):
        for delta in range(1, RANKS):
            rank = (me + delta) % RANKS
            pltpu.make_async_remote_copy(
                src_ref=out_ref.at[(rank // 8) * 2 + rank % 2 if by_owner else rank],
                dst_ref=in_ref.at[me],
                send_sem=send,
                recv_sem=recv,
                device_id=device_of(rank),
                device_id_type=MESH,
            ).start()

    def swap_whole(out_ref, in_ref, send, recv, by_owner=False):
        others = in_ref.at[pl.ds(0, RANKS - 1)]
        return pltpu.make_async_remote_copy(
            src_ref=others,
            dst_ref=others,
            send_sem=send,
            recv_sem=recv,
            device_id=device_of((me + 1) % RANKS),
            device_id_type=MESH,
        )

    into = (pack_out, pack_in, a_send, a_recv)
    swap_start(*into)
    pack_in[me] = pack_out[me]
    swap_whole(*into).wait_recv()
    put_blocks(nat, swap_bits(pack_in[...].reshape(32, 2, 8, 128), 5))

    def wide(row_value):
        return jnp.broadcast_to(row_value, (8, 128))

    bulk_l = wide(nat[0, 125:126])
    buoy_l = wide(nat[0, 126:127])
    layers_l = wide(nat[0, 127:128])
    depth = 4.0 * bits[2] + 2.0 * bits[1] + bits[5]
    strike = 4.0 * bits[4] + 2.0 * bits[3] + bits[6]
    active = jnp.where(depth < layers_l, 1.0, 0.0)
    act_k = active * k_mask

    for line in range(25):
        state[0, :, 8 * line : 8 * line + 8, :] = nat[:, 5 * line : 5 * line + 8, :] * act_k

    def face_rows(ref, field, axis, side):
        node = 4 * side
        if axis == 0:
            return ref[field, 40 * node : 40 * node + 40, :].reshape(5, 8, 128)
        return jnp.stack([ref[field, 40 * i + 8 * node : 40 * i + 8 * node + 8, :] for i in range(5)])

    def face_copy(step, number, direction):
        return pltpu.make_async_remote_copy(
            src_ref=face_out.at[step, direction, number],
            dst_ref=face_in.at[step, direction, number],
            send_sem=h_send.at[step, direction],
            recv_sem=h_recv.at[step, direction, number],
            device_id=layer(1 - 2 * direction),
            device_id_type=MESH,
        )

    def face_do(step, number, direction, work):
        @pl.when(has_above if direction == 0 else has_below)
        def _():
            work(face_copy(step, number, direction))

    def face_wait(step, number, direction):
        @pl.when(has_below if direction == 0 else has_above)
        def _():
            face_copy(step, number, direction).wait_recv()

    def pack_two(first, second, direction):
        mask = bit_mask(first.shape, 0)
        if direction == 0:
            return jnp.where(mask, second, lane_roll(first, -1))
        return jnp.where(mask, lane_roll(first, 1), second)

    def near_planes(ref):
        out = []
        for field in range(4):
            low, high = face_rows(ref, field, 1, 0), face_rows(ref, field, 1, 1)
            out.append(jnp.where(bit_mask(low.shape, 0), high, low))
        return out

    def send_planes(step, number, planes):
        for direction in range(2):
            for half, (one, two) in enumerate(((0, 2), (1, 3))):
                packed = pack_two(planes[one], planes[two], direction)
                for line in range(5):
                    at = 25 * half + 5 * line
                    face_out[step, direction, number, at : at + 8, :] = packed[line]
            if number == 0:
                extra = jnp.where(
                    sub == 5,
                    pack_two(coef[BULK], coef[BUOY], direction),
                    pack_two(coef[ACTIVE], coef[ACTIVE], direction),
                )
                face_out[step, direction, number, 48:56, :] = jnp.where(
                    sub >= 5, extra, face_out[step, direction, number, 48:56, :]
                )
            face_do(step, number, direction, start)

    def unpack_two(below, above):
        mask = bit_mask(below.shape, 0)
        return jnp.where(mask, above, below), flip(jnp.where(mask, below, above), 0)

    def arrived_planes(step, number):
        for direction in range(2):
            face_wait(step, number, direction)
        out = []
        for half in range(2):
            rows = [
                jnp.stack(
                    [
                        face_in[step, direction, number, 25 * half + 5 * line : 25 * half + 5 * line + 8, :]
                        for line in range(5)
                    ]
                )
                for direction in range(2)
            ]
            out.append(unpack_two(rows[0], rows[1]))
        return [out[0][0], out[1][0], out[0][1], out[1][1]]

    coef[BULK] = bulk_l
    coef[BUOY] = buoy_l
    coef[ACTIVE] = active
    send_planes(0, 0, near_planes(state.at[0]))

    def element_coefs(at, bulk_e, buoy_e, active_e):
        speed_e = jnp.sqrt(bulk_e * buoy_e)
        use = active_e * k_mask
        coef[at + VOL] = buoy_e * use
        coef[at + VOL + 1] = bulk_e * use
        coef[at + VOL + 2] = GRAVITY / buoy_e * use
        for number, (axis, place) in enumerate(((0, strike), (2, depth))):
            for side in range(2):
                inside = jnp.where(place > 0.5, 1.0, 0.0) if side == 0 else jnp.where(place < 6.5, 1.0, 0.0)
                sign = 1.0 if side == 1 else -1.0
                scale = 5.0 * (use if axis == 0 else active_e)
                jump = scale * jnp.maximum(speed_e, inside * neighbour_lanes(speed_e, axis, side))
                to = at + FACES + 8 * number + 4 * side
                coef[to] = jump
                coef[to + 1] = jump * inside
                coef[to + 2] = sign * scale * inside * neighbour_lanes(buoy_e, axis, side)
                coef[to + 3] = sign * scale * inside * neighbour_lanes(bulk_e, axis, side)
        return speed_e

    speed_l = element_coefs(0, bulk_l, buoy_l, active)
    coef[SPEED] = speed_l
    coef[SELECT] = jnp.where(depth == layers_l - 1.0, 1.0, 0.0)
    for side in range(2):
        use = 5.0 * act_k * (bits[0] if side == 0 else 1.0 - bits[0])
        sign = 1.0 if side == 1 else -1.0
        at = INNER + 3 * side
        coef[at] = use * jnp.maximum(speed_l, neighbour_lanes(speed_l, 1, side))
        coef[at + 1] = sign * use * neighbour_lanes(buoy_l, 1, side)
        coef[at + 2] = sign * use * neighbour_lanes(bulk_l, 1, side)

    def outer_coefs():
        packed = [
            [jnp.broadcast_to(face_in[0, direction, 0, at : at + 1, :], (8, 128)) for direction in range(2)]
            for at in (53, 54)
        ]
        bulk_o, buoy_o = unpack_two(packed[0][0], packed[0][1])
        active_o = unpack_two(packed[1][0], packed[1][1])[0]
        has_low = jnp.where(zc == 0, 0.0, 1.0).astype(jnp.float32)
        has_high = jnp.where(zc == N_ZC - 1, 0.0, 1.0).astype(jnp.float32)
        inside = has_low * (1.0 - bits[0]) + has_high * bits[0]
        buoy_o = buoy_o + (1.0 - inside)
        speed_o = element_coefs(GHOST, bulk_o, buoy_o, active_o)
        sign = 2.0 * bits[0] - 1.0
        speed = jnp.maximum(coef[SPEED], inside * speed_o)
        use = 5.0 * coef[ACTIVE] * k_mask
        coef[OUTER] = use * speed
        coef[OUTER + 1] = use * speed * inside
        coef[OUTER + 2] = use * sign * inside * buoy_o
        coef[OUTER + 3] = use * sign * inside * bulk_o
        use_o = 5.0 * active_o * k_mask * inside
        coef[INTO] = use_o * speed
        coef[INTO + 1] = use_o * speed
        coef[INTO + 2] = -sign * use_o * coef[BUOY]
        coef[INTO + 3] = -sign * use_o * coef[BULK]
        coef[INTO + 4] = KAPPA * bulk_o * buoy_o * active_o * k_mask

    def row(index):
        return coef[index, 0:1, :]

    def rates(src, dst, planes, base):
        def cube(field):
            return src[field].reshape(5, planes, 8, 128)

        def along_i(value):
            return jnp.stack([weighted(TABLE[i], [value[m] for m in range(5)]) for i in range(5)])

        def along_j(value):
            return jnp.stack(
                [weighted(TABLE[j], [value[:, m] for m in range(5)]) for j in range(5)], axis=1
            )

        def along_k(value):
            total = None
            for node in range(5):
                one = jnp.broadcast_to(value[:, :, node : node + 1, :], value.shape)
                term = coef[COL_D + node] * one
                total = term if total is None else total + term
            return total

        def put(field, value):
            dst[field] = value.reshape(40 * planes, 128)

        vol_b, vol_k, vol_g = coef[base + VOL], coef[base + VOL + 1], coef[base + VOL + 2]
        pressure = cube(0)
        put(1, vol_k * along_i(pressure))
        put(2, vol_k * along_j(pressure) if planes == 5 else jnp.zeros_like(pressure))
        put(3, vol_k * along_k(pressure) + vol_g * pressure)
        total = along_i(cube(1)) + along_k(cube(3))
        if planes == 5:
            total = total + along_j(cube(2))
        put(0, vol_b * total)

        size = 8 * planes

        def x_face(ref, field, side):
            return ref[field, 4 * size * side : 4 * size * side + size, :].reshape(planes, 8, 128)

        for side in range(2):
            at = base + FACES + 4 * side
            outer = [neighbour_lanes(x_face(src, field, 1 - side), 0, side) for field in range(4)]
            for field in range(4):
                add = coef[at + 1] * outer[field] - coef[at] * x_face(src, field, side)
                if field == 0:
                    add = add + coef[at + 2] * outer[1]
                if field == 1:
                    add = add + coef[at + 3] * outer[0]
                rows = slice(4 * size * side, 4 * size * side + size)
                dst[field, rows, :] = dst[field, rows, :] + add.reshape(size, 128)

        if planes == 5:
            for side in range(2):
                at = INNER + 3 * side
                outer = [neighbour_lanes(face_rows(src, field, 1, 1 - side), 1, side) for field in range(4)]
                for field in range(4):
                    add = coef[at] * (outer[field] - face_rows(src, field, 1, side))
                    if field == 0:
                        add = add + coef[at + 1] * outer[2]
                    if field == 2:
                        add = add + coef[at + 2] * outer[0]
                    for i in range(5):
                        rows = slice(40 * i + 32 * side, 40 * i + 32 * side + 8)
                        dst[field, rows, :] = dst[field, rows, :] + add[i]

        lines = [[src[field, pl.ds(4 * side, 5 * planes, stride=8), :] for field in range(4)] for side in range(2)]
        for side in range(2):
            at = base + FACES + 8 + 4 * side
            outer = [neighbour_lanes(lines[1 - side][field], 2, side) for field in range(4)]
            for field in range(4):
                add = row(at + 1) * outer[field] - row(at) * lines[side][field]
                if field == 0:
                    add = add + row(at + 2) * outer[3]
                if field == 3:
                    add = add + row(at + 3) * outer[0]
                where = pl.ds(4 * side, 5 * planes, stride=8)
                dst[field, where, :] = dst[field, where, :] + add

    def flux(at, other, own):
        out = [coef[at + 1] * other[field] - coef[at] * own[field] for field in range(4)]
        out[0] = out[0] + coef[at + 2] * other[2]
        out[2] = out[2] + coef[at + 3] * other[0]
        return out

    def add_outer(ref, adds, scale):
        for field in range(4):
            add = scale * adds[field]
            mask = bit_mask(add.shape, 0)
            low, high = jnp.where(mask, 0.0, add), jnp.where(mask, add, 0.0)
            for i in range(5):
                for part, at in ((low, 40 * i), (high, 40 * i + 32)):
                    ref[field, at : at + 8, :] = ref[field, at : at + 8, :] + part[i]

    def add_floor(ref, share):
        for field in range(4):
            floor[field] += share * ref[field, pl.ds(4, 25, stride=8), :]

    def trace_copy(steps, labels=False):
        part = 2 * (steps - 1) + (1 if labels else 0)
        return pltpu.make_async_remote_copy(
            src_ref=label_out if labels else tr_out,
            dst_ref=(label_in if labels else tr_in).at[steps - 1],
            send_sem=t_send.at[part],
            recv_sem=t_recv.at[part],
            device_id=layer(steps),
            device_id_type=MESH,
        )

    def send_floor():
        chosen = [floor[field] * row(SELECT) for field in range(4)]
        pair = [fold_pair(chosen[0], chosen[1], 1), fold_pair(chosen[2], chosen[3], 1)]
        together = fold_pair(pair[0], pair[1], 2)
        tr_out[0:25] = together + flip(together, 5)
        tr_out[25:32] = jnp.zeros((7, 128), jnp.float32)
        for steps in (1, 2):
            trace_copy(steps).start()

    def as_planes(ref):
        return [ref[field].reshape(5, 8, 128) for field in range(4)]

    def put_planes(ref, planes):
        for field in range(4):
            ref[field] = planes[field].reshape(40, 128)

    half, sixth, third = DT / 2.0, DT / 6.0, DT / 3.0
    now, first, second, third_in = state.at[0], state.at[1], state.at[2], state.at[3]

    def time_step(step, carry):
        add_floor(now, sixth)
        rates(now, rate, 5, 0)
        for field in range(4):
            first[field] = now[field] + half * rate[field]
            update[field] = sixth * rate[field]
        send_planes(step, 1, near_planes(first))
        rates(first, rate, 5, 0)
        for field in range(4):
            second[field] = now[field] + half * rate[field]
            update[field] = update[field] + third * rate[field]
        planes = near_planes(second)
        send_planes(step, 2, planes)
        put_planes(near, planes)
        rates(near, ghost_rate, 1, 0)

        def across(field):
            value = second[field].reshape(5, 5, 8, 128)
            parts = [value[:, m] for m in range(5)]
            low, high = weighted(TABLE[0], parts), weighted(TABLE[4], parts)
            return jnp.where(bit_mask(low.shape, 0), high, low)

        slopes = as_planes(ghost_rate)
        slopes[0] = slopes[0] + coef[VOL] * across(2)
        slopes[2] = slopes[2] + coef[VOL + 1] * across(0)
        starts = near_planes(now)
        send_planes(step, 3, [starts[field] + DT * slopes[field] for field in range(4)])

        outer = arrived_planes(step, 0)

        @pl.when(step == 0)
        def _():
            outer_coefs()
            label_out[...] = wide(nat[1, 125:126])
            for steps in (1, 2):
                trace_copy(steps, True).start()

        own = near_planes(now)
        adds = flux(OUTER, outer, own)
        add_outer(first, adds, half)
        add_outer(update, adds, sixth)
        answer = [half * term for term in flux(INTO, own, outer)]
        put_planes(ghost.at[0], answer)
        free = arrived_planes(step, 1)
        outer = [free[field] + answer[field] for field in range(4)]

        add_floor(first, third)
        own = near_planes(first)
        came = [half * add for add in adds]
        put_planes(near, came)
        rates(near, ghost_rate, 1, 0)
        slopes = as_planes(ghost_rate)
        adds = [slopes[field] + term for field, term in enumerate(flux(OUTER, outer, own))]
        add_outer(second, adds, half)
        add_outer(update, adds, third)
        for field, source, scale in ((0, 2, coef[VOL]), (2, 0, coef[VOL + 1])):
            inward = scale * came[source]
            for j in range(5):
                weight = jnp.where((lane & 1) != 0, float(TABLE[j, 4]), float(TABLE[j, 0]))
                term = weight * inward
                for i in range(5):
                    at = 40 * i + 8 * j
                    second[field, at : at + 8, :] = second[field, at : at + 8, :] + half * term[i]
                    update[field, at : at + 8, :] = update[field, at : at + 8, :] + third * term[i]
        rates(ghost.at[0], ghost_rate, 1, GHOST)
        slopes = as_planes(ghost_rate)
        answer = [half * (slopes[field] + term) for field, term in enumerate(flux(INTO, own, outer))]
        put_planes(ghost.at[1], answer)
        free = arrived_planes(step, 2)
        outer = [free[field] + answer[field] for field in range(4)]

        add_floor(second, third)
        rates(second, rate, 5, 0)
        own = near_planes(second)
        adds = flux(OUTER, outer, own)
        for field in range(4):
            third_in[field] = now[field] + DT * rate[field]
            update[field] = update[field] + third * rate[field]
        add_outer(third_in, adds, DT)
        add_outer(update, adds, third)
        rates(ghost.at[1], ghost_rate, 1, GHOST)
        slopes = as_planes(ghost_rate)
        early = as_planes(ghost.at[0])
        for field in (0, 2):
            slopes[field] = slopes[field] + half * (coef[INTO + 4] * early[field])
        answer = [DT * (slopes[field] + term) for field, term in enumerate(flux(INTO, own, outer))]
        free = arrived_planes(step, 3)
        outer = [free[field] + answer[field] for field in range(4)]

        add_floor(third_in, sixth)

        @pl.when(step == STEPS - 1)
        def _():
            send_floor()

        rates(third_in, rate, 5, 0)
        adds = flux(OUTER, outer, near_planes(third_in))
        for field in range(4):
            now[field] = now[field] + update[field] + sixth * rate[field]
        add_outer(now, adds, sixth)

        @pl.when(step < STEPS - 1)
        def _():
            send_planes(step + 1, 0, near_planes(now))

        return carry

    lax.fori_loop(0, STEPS, time_step, 0)

    for line in range(25):
        nat[:, 5 * line : 5 * line + 8, :] = now[:, 8 * line : 8 * line + 8, :]
    back_out[...] = swap_bits(blocks_of(nat), 5).reshape(32, 16, 128)
    back = (back_out, back_in, b_send, b_recv)
    swap_start(*back)
    back_in[me] = back_out[me]

    for steps in (1, 2):
        trace_copy(steps, True).wait_recv()
    from_lane = lax.broadcasted_iota(jnp.int32, (128, 128), 0)
    to_lane = lax.broadcasted_iota(jnp.int32, (128, 128), 1)
    same_field = ((from_lane // 2) % 4 == to_lane // 32) & ((from_lane // 32) % 2 == 0)
    for at, source in enumerate((label_out, label_in.at[0], label_in.at[1])):
        label = jnp.transpose(jnp.broadcast_to(source[0:1], (128, 128))).astype(jnp.int32)
        for upper in range(2):
            owner = (upper * 2 + (to_lane // 2) % 2) * (2 * N_ZC) + 2 * zc + to_lane % 2
            cell = owner * S_DEV + (to_lane // 4) % 8
            chosen[128 * at : 128 * at + 128, 128 * upper : 128 * upper + 128] = jnp.where(
                same_field & (label == cell), 1.0, 0.0
            )
    for steps in (1, 2):
        trace_copy(steps).wait_recv()
    total = jnp.dot(
        jnp.concatenate([tr_out[...], tr_in[0], tr_in[1]], axis=1), chosen[...],
        precision=lax.Precision.HIGHEST, preferred_element_type=jnp.float32,
    )
    for upper in range(2):
        part = total[:, 128 * upper : 128 * upper + 128]
        tb_out[4 * upper : 4 * upper + 4] = swap_bits(part.reshape(4, 8, 128), 2)
    ends = (tb_out, tb_in, c_send, c_recv, True)
    swap_start(*ends)
    tb_in[me] = tb_out[gx * 2 + y_lo]

    swap_whole(*back).wait_recv()
    put_blocks(nat, swap_bits(back_in[...].reshape(32, 2, 8, 128), 5))
    elements = field_swap([nat[field, 0:125] for field in range(4)])
    for e in range(4):
        out[e // 2, 0, :, e % 2, :] = elements[e]

    swap_whole(*ends).wait_recv()
    sums = swap_bits(tb_in[...], 5).reshape(8, 32, 128)
    for cell in range(S_DEV):
        trace[pl.ds(cell, 25, stride=8), :] = sums[cell, 0:25]

    for swap in (into, back, ends):
        swap_whole(*swap).wait_send()
    for steps in (1, 2):
        trace_copy(steps).wait_send()
        trace_copy(steps, True).wait_send()

    def drain(step, carry):
        for direction in range(2):
            sent = face_out.at[step, direction]

            @pl.when(has_above if direction == 0 else has_below)
            def _():
                pltpu.make_async_remote_copy(
                    src_ref=sent,
                    dst_ref=face_in.at[step, direction],
                    send_sem=h_send.at[step, direction],
                    recv_sem=h_recv.at[step, direction, 0],
                    device_id=layer(1 - 2 * direction),
                    device_id_type=MESH,
                ).wait_send()

        return carry

    lax.fori_loop(0, STEPS, drain, 0)


def shards(adjoint_state, bulk_modulus, buoyancy, water_layers, surface_cell):
    f32 = jnp.float32
    in_any = pl.BlockSpec(memory_space=pl.ANY)
    dma = pltpu.SemaphoreType.DMA
    by_node = jnp.transpose(adjoint_state, (0, 1, 3, 2, 4))
    out, trace = pl.pallas_call(
        kernel,
        out_shape=(
            jax.ShapeDtypeStruct(by_node.shape, f32),
            jax.ShapeDtypeStruct((S_DEV * 25, 128), f32),
        ),
        in_specs=[in_any] * 5,
        out_specs=(pl.BlockSpec(memory_space=pltpu.VMEM),) * 2,
        scratch_shapes=[
            pltpu.SMEM(bulk_modulus.shape, f32),
            pltpu.SMEM(buoyancy.shape, f32),
            pltpu.SMEM(water_layers.T.shape, jnp.int32),
            pltpu.SMEM(surface_cell.T.shape, jnp.int32),
            pltpu.VMEM(by_node.shape, f32),
            pltpu.VMEM((4, 128, 128), f32),
            pltpu.VMEM((32, 16, 128), f32),
            pltpu.VMEM((32, 16, 128), f32),
            pltpu.VMEM((32, 16, 128), f32),
            pltpu.VMEM((32, 16, 128), f32),
            pltpu.VMEM((4, 4, 200, 128), f32),
            pltpu.VMEM((4, 200, 128), f32),
            pltpu.VMEM((4, 200, 128), f32),
            pltpu.VMEM((N_COEF, 8, 128), f32),
            pltpu.VMEM((4, 40, 128), f32),
            pltpu.VMEM((2, 4, 40, 128), f32),
            pltpu.VMEM((4, 40, 128), f32),
            pltpu.VMEM((STEPS, 2, 4, 56, 128), f32),
            pltpu.VMEM((STEPS, 2, 4, 56, 128), f32),
            pltpu.VMEM((4, 25, 128), f32),
            pltpu.VMEM((32, 128), f32),
            pltpu.VMEM((2, 32, 128), f32),
            pltpu.VMEM((8, 128), f32),
            pltpu.VMEM((2, 8, 128), f32),
            pltpu.VMEM((384, 256), f32),
            pltpu.VMEM((8, 8, 128), f32),
            pltpu.VMEM((32, 8, 128), f32),
            dma((5,)),
            dma,
            dma,
            dma((STEPS, 2)),
            dma((STEPS, 2, 4)),
            dma((4,)),
            dma((4,)),
            dma,
            dma,
            dma,
            dma,
        ],
        compiler_params=pltpu.CompilerParams(
            collective_id=0, has_side_effects=True, vmem_limit_bytes=54656 * 1024
        ),
        name="adjoint_steps",
    )(by_node, bulk_modulus, buoyancy, water_layers.T, surface_cell.T)
    return (
        jnp.transpose(out, (0, 1, 3, 2, 4)),
        jnp.transpose(trace.reshape(25, S_DEV, 128), (1, 0, 2)),
    )


def solution(mesh):
    placed = (
        P("gx", "gy", "gz", None, None),
        P("gx", "gy", "gz"),
        P("gx", "gy", "gz"),
        P("gx", "gy"),
        P("gx", "gy"),
    )
    return jax.shard_map(
        shards,
        mesh=mesh,
        in_specs=placed,
        out_specs=(P("gx", "gy", "gz", None, None), P(("gx", "gy"), None, None)),
        check_vma=False,
    )
```

```python
import math

import jax
import jax.numpy as jnp
import numpy as np
from jax import lax
from jax.experimental import pallas as pl
from jax.experimental.pallas import tpu as pltpu
from jax.sharding import PartitionSpec as P

N_ZC = 8
RANKS = 32
STEPS = 2
S_DEV = 8
GRAVITY = 2.0
DT = 0.02
MESH = pl.DeviceIdType.MESH


def derivative_rows():
    points = np.array([-1.0, -math.sqrt(3.0 / 7.0), 0.0, math.sqrt(3.0 / 7.0), 1.0])
    scales = np.array(
        [np.prod([points[a] - points[b] for b in range(5) if b != a]) for a in range(5)]
    )
    table = np.zeros((5, 5))
    for a in range(5):
        for b in range(5):
            if a != b:
                table[a, b] = scales[a] / scales[b] / (points[a] - points[b])
        table[a, a] = -np.sum(table[a])
    table[0, 0] += 5.0
    table[4, 4] -= 5.0
    table[np.abs(table) < 1e-12] = 0.0
    return table


TABLE = derivative_rows()
KAPPA = float(np.dot(TABLE[0], TABLE[:, 0]))


def weighted(row, parts):
    total = None
    for weight, part in zip(row, parts):
        if weight != 0.0:
            term = float(weight) * part
            total = term if total is None else total + term
    return total


def bit_mask(shape, bit):
    lanes = lax.broadcasted_iota(jnp.int32, shape, len(shape) - 1)
    return (lanes & (1 << bit)) != 0


def lane_roll(value, shift):
    return pltpu.roll(value, shift % 128, axis=value.ndim - 1)


def swap_pair(low, high, bit):
    width = 1 << bit
    mask = bit_mask(low.shape, bit)
    return (
        jnp.where(mask, lane_roll(high, width), low),
        jnp.where(mask, high, lane_roll(low, -width)),
    )


def swap_stage(value, index_bit, lane_bit):
    step = 1 << index_bit
    shape = value.shape
    split = value.reshape((shape[0] // (2 * step), 2, step) + shape[1:])
    part = split[:, 0].shape
    flat = (-1,) + shape[-2:]
    low, high = swap_pair(split[:, 0].reshape(flat), split[:, 1].reshape(flat), lane_bit)
    return jnp.stack([low.reshape(part), high.reshape(part)], axis=1).reshape(shape)


def swap_bits(value, count):
    for bit in range(count):
        value = swap_stage(value, bit, bit)
    return value


def flip(value, bit):
    width = 1 << bit
    mask = bit_mask(value.shape, bit)
    return jnp.where(mask, lane_roll(value, width), lane_roll(value, -width))


def fold_pair(low, high, bit):
    mask = bit_mask(low.shape, bit)
    return jnp.where(mask, high, low) + flip(jnp.where(mask, low, high), bit)


def neighbour_lanes(value, axis, side):
    if axis == 1:
        return lane_roll(value, 1 if side == 0 else -1)
    wide, short, bit = (64, 56, 6) if axis == 0 else (32, 30, 5)
    mask = bit_mask(value.shape, bit)
    if side == 0:
        return jnp.where(mask, lane_roll(value, wide), lane_roll(value, -short))
    return jnp.where(mask, lane_roll(value, short), lane_roll(value, -wide))


def hops(turn, mask):
    return min(turn, 4 - turn) + {0: 0, 1: 1, 4: 2, 5: 1}[mask & 5]


FAR_FIRST = sorted(
    ((turn, mask) for turn in range(4) for mask in range(8) if turn or mask),
    key=lambda pair: (-hops(*pair), pair[1] & 5, pair[0]),
)

VOL = 0
FACES = 3
SET = 19
GHOST = SET
INNER = 2 * SET
OUTER = INNER + 6
INTO = OUTER + 4
COL_D = INTO + 5
SELECT = COL_D + 5
BULK, BUOY, ACTIVE, SPEED = SELECT + 1, SELECT + 2, SELECT + 3, SELECT + 4
N_COEF = SPEED + 1


def kernel(
    state_hbm, bulk_hbm, buoy_hbm, layers_hbm, cells_hbm, out, trace,
    bulk, buoy, layers, cells,
    staged, nat, pack_out, pack_in, back_out, back_in, state, update, rate, coef,
    near, ghost, ghost_rate, face_out, face_in, floor, tr_out, tr_in, label_out, label_in, chosen, tb_out, tb_in,
    local_sem, a_send, a_recv, h_send, h_recv, t_send, t_recv, b_send, b_recv, c_send, c_recv,
):
    gx = lax.axis_index("gx")
    gy = lax.axis_index("gy")
    gz = lax.axis_index("gz")
    zc, y_lo = gy // 2, gy % 2
    me = gx * 8 + gz * 2 + y_lo

    load = pltpu.make_async_copy(state_hbm, staged, local_sem.at[0])
    load.start()
    small = [
        pltpu.make_async_copy(source, target, local_sem.at[1 + at])
        for at, (source, target) in enumerate(
            ((bulk_hbm, bulk), (buoy_hbm, buoy), (layers_hbm, layers), (cells_hbm, cells))
        )
    ]
    for copy in small:
        copy.start()

    def device_of(rank):
        return (rank // 8, zc * 2 + rank % 2, (rank // 2) % 4)

    def layer(steps):
        return (gx, (gy + 2 * steps + 2 * N_ZC) % (2 * N_ZC), gz)

    barrier = pltpu.get_barrier_semaphore()

    has_below, has_above = zc > 0, zc < N_ZC - 1

    def greet(device):
        pl.semaphore_signal(barrier, inc=1, device_id=device, device_id_type=MESH)

    for delta in range(1, RANKS):
        greet(device_of((me + delta) % RANKS))

    @pl.when(has_below)
    def _():
        greet(layer(-1))

    @pl.when(has_above)
    def _():
        greet(layer(1))

    @pl.when(zc == 0)
    def _():
        greet(layer(-1))
        greet(layer(-2))

    @pl.when(zc == 1)
    def _():
        greet(layer(-2))

    greetings = (
        RANKS - 1
        + has_below.astype(jnp.int32)
        + has_above.astype(jnp.int32)
        + (zc == N_ZC - 2).astype(jnp.int32)
        + 2 * (zc == N_ZC - 1).astype(jnp.int32)
    )

    floor[...] = jnp.zeros_like(floor)
    face_out[...] = jnp.zeros_like(face_out)

    @pl.when(zc == 0)
    def _():
        face_in[:, 0] = jnp.zeros((STEPS, 4, 56, 128), jnp.float32)

    @pl.when(zc == N_ZC - 1)
    def _():
        face_in[:, 1] = jnp.zeros((STEPS, 4, 56, 128), jnp.float32)

    sub = lax.broadcasted_iota(jnp.int32, (8, 128), 0)
    lane = lax.broadcasted_iota(jnp.int32, (8, 128), 1)
    bits = [jnp.where((lane & (1 << bit)) != 0, 1.0, 0.0) for bit in range(7)]
    k_mask = jnp.where(sub < 5, 1.0, 0.0)
    for node in range(5):
        column = jnp.zeros((8, 128), jnp.float32)
        for row_at in range(5):
            if TABLE[row_at, node] != 0.0:
                column = jnp.where(sub == row_at, float(TABLE[row_at, node]), column)
        coef[COL_D + node] = column

    lane1 = lax.broadcasted_iota(jnp.int32, (1, 128), 1)
    high1 = (lane1 & 64) != 0
    low1 = (lane1 & 32) != 0

    def element_row(ref):
        return jnp.where(
            high1,
            jnp.where(low1, ref[1, 0, 1], ref[1, 0, 0]),
            jnp.where(low1, ref[0, 0, 1], ref[0, 0, 0]),
        )

    def column_row(ref):
        return jnp.where(high1, ref[0, 1].astype(jnp.float32), ref[0, 0].astype(jnp.float32))

    def blocks_of(ref):
        return jnp.stack(
            [
                jnp.stack([ref[low, 8 * tile : 8 * tile + 8], ref[2 + low, 8 * tile : 8 * tile + 8]])
                for tile in range(16)
                for low in range(2)
            ]
        )

    def put_blocks(ref, value):
        for at in range(32):
            tile, low = at // 2, at % 2
            for high in range(2):
                ref[2 * high + low, 8 * tile : 8 * tile + 8] = value[at, high]

    def field_swap(parts):
        for step, bit in ((1, 5), (2, 6)):
            for at in range(4):
                if not at & step:
                    parts[at], parts[at + step] = swap_pair(parts[at], parts[at + step], bit)
        return parts

    load.wait()
    for copy in small:
        copy.wait()
    fields = field_swap([staged[e // 2, 0, :, e % 2, :] for e in range(4)])
    for field in range(4):
        nat[field, 0:125] = fields[field]
    nat[0, 125:126] = element_row(bulk)
    nat[0, 126:127] = element_row(buoy)
    nat[0, 127:128] = column_row(layers)
    cell_row = column_row(cells)
    nat[1, 125:126] = cell_row
    nat[1, 126:127] = cell_row
    nat[1, 127:128] = cell_row
    for field in (2, 3):
        nat[field, 125:128] = jnp.zeros((3, 128), jnp.float32)
    pack_out[...] = swap_bits(blocks_of(nat), 5).reshape(32, 16, 128)

    pl.semaphore_wait(barrier, greetings)

    def start(copy):
        copy.start()

    def leave(copy):
        copy.wait_send()

    def swap_start(out_ref, in_ref, send, recv, by_owner=False):
        for turn, mask in FAR_FIRST:
            low = [(me // (1 << b)) % 2 for b in range(3)]
            low = [1 - v if mask & (1 << b) else v for b, v in enumerate(low)]
            rank = ((gx + turn) % 4) * 8 + low[2] * 4 + low[1] * 2 + low[0]
            pltpu.make_async_remote_copy(
                src_ref=out_ref.at[(rank // 8) * 2 + rank % 2 if by_owner else rank],
                dst_ref=in_ref.at[me],
                send_sem=send,
                recv_sem=recv,
                device_id=device_of(rank),
                device_id_type=MESH,
            ).start()

    def swap_whole(out_ref, in_ref, send, recv, by_owner=False):
        others = in_ref.at[pl.ds(0, RANKS - 1)]
        return pltpu.make_async_remote_copy(
            src_ref=others,
            dst_ref=others,
            send_sem=send,
            recv_sem=recv,
            device_id=device_of((me + 1) % RANKS),
            device_id_type=MESH,
        )

    into = (pack_out, pack_in, a_send, a_recv)
    swap_start(*into)
    pack_in[me] = pack_out[me]
    swap_whole(*into).wait_recv()
    put_blocks(nat, swap_bits(pack_in[...].reshape(32, 2, 8, 128), 5))

    def wide(row_value):
        return jnp.broadcast_to(row_value, (8, 128))

    bulk_l = wide(nat[0, 125:126])
    buoy_l = wide(nat[0, 126:127])
    layers_l = wide(nat[0, 127:128])
    depth = 4.0 * bits[2] + 2.0 * bits[1] + bits[5]
    strike = 4.0 * bits[4] + 2.0 * bits[3] + bits[6]
    active = jnp.where(depth < layers_l, 1.0, 0.0)
    act_k = active * k_mask

    for line in range(25):
        state[0, :, 8 * line : 8 * line + 8, :] = nat[:, 5 * line : 5 * line + 8, :] * act_k

    def face_rows(ref, field, axis, side):
        node = 4 * side
        if axis == 0:
            return ref[field, 40 * node : 40 * node + 40, :].reshape(5, 8, 128)
        return jnp.stack([ref[field, 40 * i + 8 * node : 40 * i + 8 * node + 8, :] for i in range(5)])

    def face_copy(step, number, direction):
        return pltpu.make_async_remote_copy(
            src_ref=face_out.at[step, direction, number],
            dst_ref=face_in.at[step, direction, number],
            send_sem=h_send.at[step, direction],
            recv_sem=h_recv.at[step, direction, number],
            device_id=layer(1 - 2 * direction),
            device_id_type=MESH,
        )

    def face_do(step, number, direction, work):
        @pl.when(has_above if direction == 0 else has_below)
        def _():
            work(face_copy(step, number, direction))

    def face_wait(step, number, direction):
        @pl.when(has_below if direction == 0 else has_above)
        def _():
            face_copy(step, number, direction).wait_recv()

    def pack_two(first, second, direction):
        mask = bit_mask(first.shape, 0)
        if direction == 0:
            return jnp.where(mask, second, lane_roll(first, -1))
        return jnp.where(mask, lane_roll(first, 1), second)

    def near_planes(ref):
        out = []
        for field in range(4):
            low, high = face_rows(ref, field, 1, 0), face_rows(ref, field, 1, 1)
            out.append(jnp.where(bit_mask(low.shape, 0), high, low))
        return out

    def send_planes(step, number, planes):
        for direction in range(2):
            for half, (one, two) in enumerate(((0, 2), (1, 3))):
                packed = pack_two(planes[one], planes[two], direction)
                for line in range(5):
                    at = 25 * half + 5 * line
                    face_out[step, direction, number, at : at + 8, :] = packed[line]
            if number == 0:
                extra = jnp.where(
                    sub == 5,
                    pack_two(coef[BULK], coef[BUOY], direction),
                    pack_two(coef[ACTIVE], coef[ACTIVE], direction),
                )
                face_out[step, direction, number, 48:56, :] = jnp.where(
                    sub >= 5, extra, face_out[step, direction, number, 48:56, :]
                )
            face_do(step, number, direction, start)

    def unpack_two(below, above):
        mask = bit_mask(below.shape, 0)
        return jnp.where(mask, above, below), flip(jnp.where(mask, below, above), 0)

    def arrived_planes(step, number):
        for direction in range(2):
            face_wait(step, number, direction)
        out = []
        for half in range(2):
            rows = [
                jnp.stack(
                    [
                        face_in[step, direction, number, 25 * half + 5 * line : 25 * half + 5 * line + 8, :]
                        for line in range(5)
                    ]
                )
                for direction in range(2)
            ]
            out.append(unpack_two(rows[0], rows[1]))
        return [out[0][0], out[1][0], out[0][1], out[1][1]]

    coef[BULK] = bulk_l
    coef[BUOY] = buoy_l
    coef[ACTIVE] = active
    send_planes(0, 0, near_planes(state.at[0]))

    def element_coefs(at, bulk_e, buoy_e, active_e):
        speed_e = jnp.sqrt(bulk_e * buoy_e)
        use = active_e * k_mask
        coef[at + VOL] = buoy_e * use
        coef[at + VOL + 1] = bulk_e * use
        coef[at + VOL + 2] = GRAVITY / buoy_e * use
        for number, (axis, place) in enumerate(((0, strike), (2, depth))):
            for side in range(2):
                inside = jnp.where(place > 0.5, 1.0, 0.0) if side == 0 else jnp.where(place < 6.5, 1.0, 0.0)
                sign = 1.0 if side == 1 else -1.0
                scale = 5.0 * (use if axis == 0 else active_e)
                jump = scale * jnp.maximum(speed_e, inside * neighbour_lanes(speed_e, axis, side))
                to = at + FACES + 8 * number + 4 * side
                coef[to] = jump
                coef[to + 1] = jump * inside
                coef[to + 2] = sign * scale * inside * neighbour_lanes(buoy_e, axis, side)
                coef[to + 3] = sign * scale * inside * neighbour_lanes(bulk_e, axis, side)
        return speed_e

    speed_l = element_coefs(0, bulk_l, buoy_l, active)
    coef[SPEED] = speed_l
    coef[SELECT] = jnp.where(depth == layers_l - 1.0, 1.0, 0.0)
    for side in range(2):
        use = 5.0 * act_k * (bits[0] if side == 0 else 1.0 - bits[0])
        sign = 1.0 if side == 1 else -1.0
        at = INNER + 3 * side
        coef[at] = use * jnp.maximum(speed_l, neighbour_lanes(speed_l, 1, side))
        coef[at + 1] = sign * use * neighbour_lanes(buoy_l, 1, side)
        coef[at + 2] = sign * use * neighbour_lanes(bulk_l, 1, side)

    def outer_coefs():
        packed = [
            [jnp.broadcast_to(face_in[0, direction, 0, at : at + 1, :], (8, 128)) for direction in range(2)]
            for at in (53, 54)
        ]
        bulk_o, buoy_o = unpack_two(packed[0][0], packed[0][1])
        active_o = unpack_two(packed[1][0], packed[1][1])[0]
        has_low = jnp.where(zc == 0, 0.0, 1.0).astype(jnp.float32)
        has_high = jnp.where(zc == N_ZC - 1, 0.0, 1.0).astype(jnp.float32)
        inside = has_low * (1.0 - bits[0]) + has_high * bits[0]
        buoy_o = buoy_o + (1.0 - inside)
        speed_o = element_coefs(GHOST, bulk_o, buoy_o, active_o)
        sign = 2.0 * bits[0] - 1.0
        speed = jnp.maximum(coef[SPEED], inside * speed_o)
        use = 5.0 * coef[ACTIVE] * k_mask
        coef[OUTER] = use * speed
        coef[OUTER + 1] = use * speed * inside
        coef[OUTER + 2] = use * sign * inside * buoy_o
        coef[OUTER + 3] = use * sign * inside * bulk_o
        use_o = 5.0 * active_o * k_mask * inside
        coef[INTO] = use_o * speed
        coef[INTO + 1] = use_o * speed
        coef[INTO + 2] = -sign * use_o * coef[BUOY]
        coef[INTO + 3] = -sign * use_o * coef[BULK]
        coef[INTO + 4] = KAPPA * bulk_o * buoy_o * active_o * k_mask

    def row(index):
        return coef[index, 0:1, :]

    def rates(src, dst, planes, base):
        def cube(field):
            return src[field].reshape(5, planes, 8, 128)

        def along_i(value):
            return jnp.stack([weighted(TABLE[i], [value[m] for m in range(5)]) for i in range(5)])

        def along_j(value):
            return jnp.stack(
                [weighted(TABLE[j], [value[:, m] for m in range(5)]) for j in range(5)], axis=1
            )

        def along_k(value):
            total = None
            for node in range(5):
                one = jnp.broadcast_to(value[:, :, node : node + 1, :], value.shape)
                term = coef[COL_D + node] * one
                total = term if total is None else total + term
            return total

        def put(field, value):
            dst[field] = value.reshape(40 * planes, 128)

        vol_b, vol_k, vol_g = coef[base + VOL], coef[base + VOL + 1], coef[base + VOL + 2]
        pressure = cube(0)
        put(1, vol_k * along_i(pressure))
        put(2, vol_k * along_j(pressure) if planes == 5 else jnp.zeros_like(pressure))
        put(3, vol_k * along_k(pressure) + vol_g * pressure)
        total = along_i(cube(1)) + along_k(cube(3))
        if planes == 5:
            total = total + along_j(cube(2))
        put(0, vol_b * total)

        size = 8 * planes

        def x_face(ref, field, side):
            return ref[field, 4 * size * side : 4 * size * side + size, :].reshape(planes, 8, 128)

        for side in range(2):
            at = base + FACES + 4 * side
            outer = [neighbour_lanes(x_face(src, field, 1 - side), 0, side) for field in range(4)]
            for field in range(4):
                add = coef[at + 1] * outer[field] - coef[at] * x_face(src, field, side)
                if field == 0:
                    add = add + coef[at + 2] * outer[1]
                if field == 1:
                    add = add + coef[at + 3] * outer[0]
                rows = slice(4 * size * side, 4 * size * side + size)
                dst[field, rows, :] = dst[field, rows, :] + add.reshape(size, 128)

        if planes == 5:
            for side in range(2):
                at = INNER + 3 * side
                outer = [neighbour_lanes(face_rows(src, field, 1, 1 - side), 1, side) for field in range(4)]
                for field in range(4):
                    add = coef[at] * (outer[field] - face_rows(src, field, 1, side))
                    if field == 0:
                        add = add + coef[at + 1] * outer[2]
                    if field == 2:
                        add = add + coef[at + 2] * outer[0]
                    for i in range(5):
                        rows = slice(40 * i + 32 * side, 40 * i + 32 * side + 8)
                        dst[field, rows, :] = dst[field, rows, :] + add[i]

        lines = [[src[field, pl.ds(4 * side, 5 * planes, stride=8), :] for field in range(4)] for side in range(2)]
        for side in range(2):
            at = base + FACES + 8 + 4 * side
            outer = [neighbour_lanes(lines[1 - side][field], 2, side) for field in range(4)]
            for field in range(4):
                add = row(at + 1) * outer[field] - row(at) * lines[side][field]
                if field == 0:
                    add = add + row(at + 2) * outer[3]
                if field == 3:
                    add = add + row(at + 3) * outer[0]
                where = pl.ds(4 * side, 5 * planes, stride=8)
                dst[field, where, :] = dst[field, where, :] + add

    def flux(at, other, own):
        out = [coef[at + 1] * other[field] - coef[at] * own[field] for field in range(4)]
        out[0] = out[0] + coef[at + 2] * other[2]
        out[2] = out[2] + coef[at + 3] * other[0]
        return out

    def add_outer(ref, adds, scale):
        for field in range(4):
            add = scale * adds[field]
            mask = bit_mask(add.shape, 0)
            low, high = jnp.where(mask, 0.0, add), jnp.where(mask, add, 0.0)
            for i in range(5):
                for part, at in ((low, 40 * i), (high, 40 * i + 32)):
                    ref[field, at : at + 8, :] = ref[field, at : at + 8, :] + part[i]

    def add_floor(ref, share):
        for field in range(4):
            floor[field] += share * ref[field, pl.ds(4, 25, stride=8), :]

    def trace_copy(steps, labels=False):
        part = 2 * (steps - 1) + (1 if labels else 0)
        return pltpu.make_async_remote_copy(
            src_ref=label_out if labels else tr_out,
            dst_ref=(label_in if labels else tr_in).at[steps - 1],
            send_sem=t_send.at[part],
            recv_sem=t_recv.at[part],
            device_id=layer(steps),
            device_id_type=MESH,
        )

    def send_floor():
        chosen = [floor[field] * row(SELECT) for field in range(4)]
        pair = [fold_pair(chosen[0], chosen[1], 1), fold_pair(chosen[2], chosen[3], 1)]
        together = fold_pair(pair[0], pair[1], 2)
        tr_out[0:25] = together + flip(together, 5)
        tr_out[25:32] = jnp.zeros((7, 128), jnp.float32)
        for steps in (1, 2):
            trace_copy(steps).start()

    def as_planes(ref):
        return [ref[field].reshape(5, 8, 128) for field in range(4)]

    def put_planes(ref, planes):
        for field in range(4):
            ref[field] = planes[field].reshape(40, 128)

    half, sixth, third = DT / 2.0, DT / 6.0, DT / 3.0
    now, first, second, third_in = state.at[0], state.at[1], state.at[2], state.at[3]

    def time_step(step, carry):
        add_floor(now, sixth)
        rates(now, rate, 5, 0)
        for field in range(4):
            first[field] = now[field] + half * rate[field]
            update[field] = sixth * rate[field]
        send_planes(step, 1, near_planes(first))
        rates(first, rate, 5, 0)
        for field in range(4):
            second[field] = now[field] + half * rate[field]
            update[field] = update[field] + third * rate[field]
        planes = near_planes(second)
        send_planes(step, 2, planes)
        put_planes(near, planes)
        rates(near, ghost_rate, 1, 0)

        def across(field):
            value = second[field].reshape(5, 5, 8, 128)
            parts = [value[:, m] for m in range(5)]
            low, high = weighted(TABLE[0], parts), weighted(TABLE[4], parts)
            return jnp.where(bit_mask(low.shape, 0), high, low)

        slopes = as_planes(ghost_rate)
        slopes[0] = slopes[0] + coef[VOL] * across(2)
        slopes[2] = slopes[2] + coef[VOL + 1] * across(0)
        starts = near_planes(now)
        send_planes(step, 3, [starts[field] + DT * slopes[field] for field in range(4)])

        outer = arrived_planes(step, 0)

        @pl.when(step == 0)
        def _():
            outer_coefs()
            label_out[...] = wide(nat[1, 125:126])
            for steps in (1, 2):
                trace_copy(steps, True).start()

        own = near_planes(now)
        adds = flux(OUTER, outer, own)
        add_outer(first, adds, half)
        add_outer(update, adds, sixth)
        answer = [half * term for term in flux(INTO, own, outer)]
        put_planes(ghost.at[0], answer)

        add_floor(first, third)
        own = near_planes(first)
        came = [half * add for add in adds]
        put_planes(near, came)
        rates(near, ghost_rate, 1, 0)
        slopes = as_planes(ghost_rate)
        for field, source, scale in ((0, 2, coef[VOL]), (2, 0, coef[VOL + 1])):
            inward = scale * came[source]
            for j in range(5):
                weight = jnp.where((lane & 1) != 0, float(TABLE[j, 4]), float(TABLE[j, 0]))
                term = weight * inward
                for i in range(5):
                    at = 40 * i + 8 * j
                    second[field, at : at + 8, :] = second[field, at : at + 8, :] + half * term[i]
                    update[field, at : at + 8, :] = update[field, at : at + 8, :] + third * term[i]
        rates(ghost.at[0], ghost_rate, 1, GHOST)
        answered = as_planes(ghost_rate)
        free = arrived_planes(step, 1)
        outer = [free[field] + answer[field] for field in range(4)]
        adds = [slopes[field] + term for field, term in enumerate(flux(OUTER, outer, own))]
        add_outer(second, adds, half)
        add_outer(update, adds, third)
        answer = [half * (answered[field] + term) for field, term in enumerate(flux(INTO, own, outer))]
        put_planes(ghost.at[1], answer)

        add_floor(second, third)
        rates(second, rate, 5, 0)
        rates(ghost.at[1], ghost_rate, 1, GHOST)
        answered = as_planes(ghost_rate)
        for field in range(4):
            third_in[field] = now[field] + DT * rate[field]
            update[field] = update[field] + third * rate[field]
        own = near_planes(second)
        early = as_planes(ghost.at[0])
        for field in (0, 2):
            answered[field] = answered[field] + half * (coef[INTO + 4] * early[field])
        free = arrived_planes(step, 2)
        outer = [free[field] + term for field, term in enumerate(as_planes(ghost.at[1]))]
        adds = flux(OUTER, outer, own)
        add_outer(third_in, adds, DT)
        add_outer(update, adds, third)
        answer = [DT * (answered[field] + term) for field, term in enumerate(flux(INTO, own, outer))]

        add_floor(third_in, sixth)

        @pl.when(step == STEPS - 1)
        def _():
            send_floor()

        rates(third_in, rate, 5, 0)
        free = arrived_planes(step, 3)
        outer = [free[field] + answer[field] for field in range(4)]
        adds = flux(OUTER, outer, near_planes(third_in))
        for field in range(4):
            now[field] = now[field] + update[field] + sixth * rate[field]
        add_outer(now, adds, sixth)

        @pl.when(step < STEPS - 1)
        def _():
            send_planes(step + 1, 0, near_planes(now))

        return carry

    lax.fori_loop(0, STEPS, time_step, 0)

    for line in range(25):
        nat[:, 5 * line : 5 * line + 8, :] = now[:, 8 * line : 8 * line + 8, :]
    back_out[...] = swap_bits(blocks_of(nat), 5).reshape(32, 16, 128)
    back = (back_out, back_in, b_send, b_recv)
    swap_start(*back)
    back_in[me] = back_out[me]

    for steps in (1, 2):
        trace_copy(steps, True).wait_recv()
    from_lane = lax.broadcasted_iota(jnp.int32, (128, 128), 0)
    to_lane = lax.broadcasted_iota(jnp.int32, (128, 128), 1)
    same_field = ((from_lane // 2) % 4 == to_lane // 32) & ((from_lane // 32) % 2 == 0)
    for at, source in enumerate((label_out, label_in.at[0], label_in.at[1])):
        label = jnp.transpose(jnp.broadcast_to(source[0:1], (128, 128))).astype(jnp.int32)
        for upper in range(2):
            owner = (upper * 2 + (to_lane // 2) % 2) * (2 * N_ZC) + 2 * zc + to_lane % 2
            cell = owner * S_DEV + (to_lane // 4) % 8
            chosen[128 * at : 128 * at + 128, 128 * upper : 128 * upper + 128] = jnp.where(
                same_field & (label == cell), 1.0, 0.0
            ).astype(jnp.bfloat16)
    for steps in (1, 2):
        trace_copy(steps).wait_recv()
    rest = jnp.concatenate([tr_out[...], tr_in[0], tr_in[1]], axis=1)
    thirds = []
    for _ in range(3):
        thirds.append(rest.astype(jnp.bfloat16))
        rest = rest - thirds[-1].astype(jnp.float32)
    total = jnp.dot(jnp.concatenate(thirds, axis=0), chosen[...], preferred_element_type=jnp.float32)
    total = total[0:32] + (total[32:64] + total[64:96])
    for upper in range(2):
        part = total[:, 128 * upper : 128 * upper + 128]
        tb_out[4 * upper : 4 * upper + 4] = swap_bits(part.reshape(4, 8, 128), 2)
    ends = (tb_out, tb_in, c_send, c_recv, True)
    swap_start(*ends)
    tb_in[me] = tb_out[gx * 2 + y_lo]

    swap_whole(*back).wait_recv()
    put_blocks(nat, swap_bits(back_in[...].reshape(32, 2, 8, 128), 5))
    elements = field_swap([nat[field, 0:125] for field in range(4)])
    for e in range(4):
        out[e // 2, 0, :, e % 2, :] = elements[e]

    swap_whole(*ends).wait_recv()
    sums = swap_bits(tb_in[...], 5).reshape(8, 32, 128)
    for cell in range(S_DEV):
        trace[pl.ds(cell, 25, stride=8), :] = sums[cell, 0:25]

    for swap in (into, back, ends):
        swap_whole(*swap).wait_send()
    for steps in (1, 2):
        trace_copy(steps).wait_send()
        trace_copy(steps, True).wait_send()

    def drain(step, carry):
        for direction in range(2):
            sent = face_out.at[step, direction]

            @pl.when(has_above if direction == 0 else has_below)
            def _():
                pltpu.make_async_remote_copy(
                    src_ref=sent,
                    dst_ref=face_in.at[step, direction],
                    send_sem=h_send.at[step, direction],
                    recv_sem=h_recv.at[step, direction, 0],
                    device_id=layer(1 - 2 * direction),
                    device_id_type=MESH,
                ).wait_send()

        return carry

    lax.fori_loop(0, STEPS, drain, 0)


def shards(adjoint_state, bulk_modulus, buoyancy, water_layers, surface_cell):
    f32 = jnp.float32
    in_any = pl.BlockSpec(memory_space=pl.ANY)
    dma = pltpu.SemaphoreType.DMA
    by_node = jnp.transpose(adjoint_state, (0, 1, 3, 2, 4))
    in_hbm = [
        pltpu.with_memory_space_constraint(value, pltpu.HBM)
        for value in (by_node, bulk_modulus, buoyancy, water_layers.T, surface_cell.T)
    ]
    out, trace = pl.pallas_call(
        kernel,
        out_shape=(
            jax.ShapeDtypeStruct(by_node.shape, f32),
            jax.ShapeDtypeStruct((S_DEV * 25, 128), f32),
        ),
        in_specs=[in_any] * 5,
        out_specs=(pl.BlockSpec(memory_space=pltpu.VMEM),) * 2,
        scratch_shapes=[
            pltpu.SMEM(bulk_modulus.shape, f32),
            pltpu.SMEM(buoyancy.shape, f32),
            pltpu.SMEM(water_layers.T.shape, jnp.int32),
            pltpu.SMEM(surface_cell.T.shape, jnp.int32),
            pltpu.VMEM(by_node.shape, f32),
            pltpu.VMEM((4, 128, 128), f32),
            pltpu.VMEM((32, 16, 128), f32),
            pltpu.VMEM((32, 16, 128), f32),
            pltpu.VMEM((32, 16, 128), f32),
            pltpu.VMEM((32, 16, 128), f32),
            pltpu.VMEM((4, 4, 200, 128), f32),
            pltpu.VMEM((4, 200, 128), f32),
            pltpu.VMEM((4, 200, 128), f32),
            pltpu.VMEM((N_COEF, 8, 128), f32),
            pltpu.VMEM((4, 40, 128), f32),
            pltpu.VMEM((2, 4, 40, 128), f32),
            pltpu.VMEM((4, 40, 128), f32),
            pltpu.VMEM((STEPS, 2, 4, 56, 128), f32),
            pltpu.VMEM((STEPS, 2, 4, 56, 128), f32),
            pltpu.VMEM((4, 25, 128), f32),
            pltpu.VMEM((32, 128), f32),
            pltpu.VMEM((2, 32, 128), f32),
            pltpu.VMEM((8, 128), f32),
            pltpu.VMEM((2, 8, 128), f32),
            pltpu.VMEM((384, 256), jnp.bfloat16),
            pltpu.VMEM((8, 8, 128), f32),
            pltpu.VMEM((32, 8, 128), f32),
            dma((5,)),
            dma,
            dma,
            dma((STEPS, 2)),
            dma((STEPS, 2, 4)),
            dma((4,)),
            dma((4,)),
            dma,
            dma,
            dma,
            dma,
        ],
        compiler_params=pltpu.CompilerParams(
            collective_id=0, has_side_effects=True, vmem_limit_bytes=32 * 1024 * 1024
        ),
        name="adjoint_steps",
    )(*in_hbm)
    return (
        jnp.transpose(out, (0, 1, 3, 2, 4)),
        jnp.transpose(trace.reshape(25, S_DEV, 128), (1, 0, 2)),
    )


def solution(mesh):
    placed = (
        P("gx", "gy", "gz", None, None),
        P("gx", "gy", "gz"),
        P("gx", "gy", "gz"),
        P("gx", "gy"),
        P("gx", "gy"),
    )
    return jax.shard_map(
        shards,
        mesh=mesh,
        in_specs=placed,
        out_specs=(P("gx", "gy", "gz", None, None), P(("gx", "gy"), None, None)),
        check_vma=False,
    )
```

```python
import math

import jax
import jax.numpy as jnp
import numpy as np
from jax import lax
from jax.experimental import pallas as pl
from jax.experimental.pallas import tpu as pltpu
from jax.sharding import PartitionSpec as P

N_ZC = 8
RANKS = 32
STEPS = 2
S_DEV = 8
GRAVITY = 2.0
DT = 0.02
MESH = pl.DeviceIdType.MESH


def derivative_rows():
    points = np.array([-1.0, -math.sqrt(3.0 / 7.0), 0.0, math.sqrt(3.0 / 7.0), 1.0])
    scales = np.array(
        [np.prod([points[a] - points[b] for b in range(5) if b != a]) for a in range(5)]
    )
    table = np.zeros((5, 5))
    for a in range(5):
        for b in range(5):
            if a != b:
                table[a, b] = scales[a] / scales[b] / (points[a] - points[b])
        table[a, a] = -np.sum(table[a])
    table[0, 0] += 5.0
    table[4, 4] -= 5.0
    table[np.abs(table) < 1e-12] = 0.0
    return table


TABLE = derivative_rows()
KAPPA = float(np.dot(TABLE[0], TABLE[:, 0]))


def weighted(row, parts):
    total = None
    for weight, part in zip(row, parts):
        if weight != 0.0:
            term = float(weight) * part
            total = term if total is None else total + term
    return total


def bit_mask(shape, bit):
    lanes = lax.broadcasted_iota(jnp.int32, shape, len(shape) - 1)
    return (lanes & (1 << bit)) != 0


def lane_roll(value, shift):
    return pltpu.roll(value, shift % 128, axis=value.ndim - 1)


def swap_pair(low, high, bit):
    width = 1 << bit
    mask = bit_mask(low.shape, bit)
    return (
        jnp.where(mask, lane_roll(high, width), low),
        jnp.where(mask, high, lane_roll(low, -width)),
    )


def swap_stage(value, index_bit, lane_bit):
    step = 1 << index_bit
    shape = value.shape
    split = value.reshape((shape[0] // (2 * step), 2, step) + shape[1:])
    part = split[:, 0].shape
    flat = (-1,) + shape[-2:]
    low, high = swap_pair(split[:, 0].reshape(flat), split[:, 1].reshape(flat), lane_bit)
    return jnp.stack([low.reshape(part), high.reshape(part)], axis=1).reshape(shape)


def swap_bits(value, count):
    for bit in range(count):
        value = swap_stage(value, bit, bit)
    return value


def flip(value, bit):
    width = 1 << bit
    mask = bit_mask(value.shape, bit)
    return jnp.where(mask, lane_roll(value, width), lane_roll(value, -width))


def fold_pair(low, high, bit):
    mask = bit_mask(low.shape, bit)
    return jnp.where(mask, high, low) + flip(jnp.where(mask, low, high), bit)


def neighbour_lanes(value, axis, side):
    if axis == 1:
        return lane_roll(value, 1 if side == 0 else -1)
    wide, short, bit = (64, 56, 6) if axis == 0 else (32, 30, 5)
    mask = bit_mask(value.shape, bit)
    if side == 0:
        return jnp.where(mask, lane_roll(value, wide), lane_roll(value, -short))
    return jnp.where(mask, lane_roll(value, short), lane_roll(value, -wide))


def hops(turn, mask):
    return min(turn, 4 - turn) + {0: 0, 1: 1, 4: 2, 5: 1}[mask & 5]


FAR_FIRST = sorted(
    ((turn, mask) for turn in range(4) for mask in range(8) if turn or mask),
    key=lambda pair: (-hops(*pair), pair[1] & 5, pair[0]),
)

VOL = 0
FACES = 3
SET = 19
GHOST = SET
INNER = 2 * SET
OUTER = INNER + 6
INTO = OUTER + 4
COL_D = INTO + 5
SELECT = COL_D + 5
BULK, BUOY, ACTIVE, SPEED = SELECT + 1, SELECT + 2, SELECT + 3, SELECT + 4
N_COEF = SPEED + 1


def kernel(
    state_hbm, bulk_hbm, buoy_hbm, layers_hbm, cells_hbm, out, trace,
    bulk, buoy, layers, cells,
    staged, nat, pack_out, pack_in, back_out, back_in, state, rate, coef,
    near, ghost, ghost_rate, face_out, face_in, floor, tr_out, tr_in, label_out, label_in, chosen, tb_out, tb_in,
    local_sem, a_send, a_recv, h_send, h_recv, t_send, t_recv, b_send, b_recv, c_send, c_recv,
):
    gx = lax.axis_index("gx")
    gy = lax.axis_index("gy")
    gz = lax.axis_index("gz")
    zc, y_lo = gy // 2, gy % 2
    me = gx * 8 + gz * 2 + y_lo

    load = pltpu.make_async_copy(state_hbm, staged, local_sem.at[0])
    load.start()
    small = [
        pltpu.make_async_copy(source, target, local_sem.at[1 + at])
        for at, (source, target) in enumerate(
            ((bulk_hbm, bulk), (buoy_hbm, buoy), (layers_hbm, layers), (cells_hbm, cells))
        )
    ]
    for copy in small:
        copy.start()

    def device_of(rank):
        return (rank // 8, zc * 2 + rank % 2, (rank // 2) % 4)

    def layer(steps):
        return (gx, (gy + 2 * steps + 2 * N_ZC) % (2 * N_ZC), gz)

    barrier = pltpu.get_barrier_semaphore()

    has_below, has_above = zc > 0, zc < N_ZC - 1

    def greet(device):
        pl.semaphore_signal(barrier, inc=1, device_id=device, device_id_type=MESH)

    for delta in range(1, RANKS):
        greet(device_of((me + delta) % RANKS))

    @pl.when(has_below)
    def _():
        greet(layer(-1))

    @pl.when(has_above)
    def _():
        greet(layer(1))

    @pl.when(zc == 0)
    def _():
        greet(layer(-1))
        greet(layer(-2))

    @pl.when(zc == 1)
    def _():
        greet(layer(-2))

    greetings = (
        RANKS - 1
        + has_below.astype(jnp.int32)
        + has_above.astype(jnp.int32)
        + (zc == N_ZC - 2).astype(jnp.int32)
        + 2 * (zc == N_ZC - 1).astype(jnp.int32)
    )

    floor[...] = jnp.zeros_like(floor)
    face_out[...] = jnp.zeros_like(face_out)

    @pl.when(zc == 0)
    def _():
        face_in[:, 0] = jnp.zeros((STEPS, 4, 56, 128), jnp.float32)

    @pl.when(zc == N_ZC - 1)
    def _():
        face_in[:, 1] = jnp.zeros((STEPS, 4, 56, 128), jnp.float32)

    sub = lax.broadcasted_iota(jnp.int32, (8, 128), 0)
    lane = lax.broadcasted_iota(jnp.int32, (8, 128), 1)
    bits = [jnp.where((lane & (1 << bit)) != 0, 1.0, 0.0) for bit in range(7)]
    k_mask = jnp.where(sub < 5, 1.0, 0.0)
    for node in range(5):
        column = jnp.zeros((8, 128), jnp.float32)
        for row_at in range(5):
            if TABLE[row_at, node] != 0.0:
                column = jnp.where(sub == row_at, float(TABLE[row_at, node]), column)
        coef[COL_D + node] = column

    lane1 = lax.broadcasted_iota(jnp.int32, (1, 128), 1)
    high1 = (lane1 & 64) != 0
    low1 = (lane1 & 32) != 0

    def element_row(ref):
        return jnp.where(
            high1,
            jnp.where(low1, ref[1, 0, 1], ref[1, 0, 0]),
            jnp.where(low1, ref[0, 0, 1], ref[0, 0, 0]),
        )

    def column_row(ref):
        return jnp.where(high1, ref[0, 1].astype(jnp.float32), ref[0, 0].astype(jnp.float32))

    def blocks_of(ref):
        return jnp.stack(
            [
                jnp.stack([ref[low, 8 * tile : 8 * tile + 8], ref[2 + low, 8 * tile : 8 * tile + 8]])
                for tile in range(16)
                for low in range(2)
            ]
        )

    def put_blocks(ref, value):
        for at in range(32):
            tile, low = at // 2, at % 2
            for high in range(2):
                ref[2 * high + low, 8 * tile : 8 * tile + 8] = value[at, high]

    def field_swap(parts):
        for step, bit in ((1, 5), (2, 6)):
            for at in range(4):
                if not at & step:
                    parts[at], parts[at + step] = swap_pair(parts[at], parts[at + step], bit)
        return parts

    load.wait()
    for copy in small:
        copy.wait()
    fields = field_swap([staged[e // 2, 0, :, e % 2, :] for e in range(4)])
    for field in range(4):
        nat[field, 0:125] = fields[field]
    nat[0, 125:126] = element_row(bulk)
    nat[0, 126:127] = element_row(buoy)
    nat[0, 127:128] = column_row(layers)
    cell_row = column_row(cells)
    nat[1, 125:126] = cell_row
    nat[1, 126:127] = cell_row
    nat[1, 127:128] = cell_row
    for field in (2, 3):
        nat[field, 125:128] = jnp.zeros((3, 128), jnp.float32)
    pack_out[...] = swap_bits(blocks_of(nat), 5).reshape(32, 16, 128)

    pl.semaphore_wait(barrier, greetings)

    def start(copy):
        copy.start()

    def leave(copy):
        copy.wait_send()

    def swap_start(out_ref, in_ref, send, recv, by_owner=False):
        for turn, mask in FAR_FIRST:
            low = [(me // (1 << b)) % 2 for b in range(3)]
            low = [1 - v if mask & (1 << b) else v for b, v in enumerate(low)]
            rank = ((gx + turn) % 4) * 8 + low[2] * 4 + low[1] * 2 + low[0]
            pltpu.make_async_remote_copy(
                src_ref=out_ref.at[(rank // 8) * 2 + rank % 2 if by_owner else rank],
                dst_ref=in_ref.at[me],
                send_sem=send,
                recv_sem=recv,
                device_id=device_of(rank),
                device_id_type=MESH,
            ).start()

    def swap_whole(out_ref, in_ref, send, recv, by_owner=False):
        others = in_ref.at[pl.ds(0, RANKS - 1)]
        return pltpu.make_async_remote_copy(
            src_ref=others,
            dst_ref=others,
            send_sem=send,
            recv_sem=recv,
            device_id=device_of((me + 1) % RANKS),
            device_id_type=MESH,
        )

    into = (pack_out, pack_in, a_send, a_recv)
    swap_start(*into)
    pack_in[me] = pack_out[me]
    swap_whole(*into).wait_recv()
    put_blocks(nat, swap_bits(pack_in[...].reshape(32, 2, 8, 128), 5))

    def wide(row_value):
        return jnp.broadcast_to(row_value, (8, 128))

    bulk_l = wide(nat[0, 125:126])
    buoy_l = wide(nat[0, 126:127])
    layers_l = wide(nat[0, 127:128])
    depth = 4.0 * bits[2] + 2.0 * bits[1] + bits[5]
    strike = 4.0 * bits[4] + 2.0 * bits[3] + bits[6]
    active = jnp.where(depth < layers_l, 1.0, 0.0)
    act_k = active * k_mask

    for line in range(25):
        state[0, :, 8 * line : 8 * line + 8, :] = nat[:, 5 * line : 5 * line + 8, :] * act_k

    def face_rows(ref, field, axis, side):
        node = 4 * side
        if axis == 0:
            return ref[field, 40 * node : 40 * node + 40, :].reshape(5, 8, 128)
        return jnp.stack([ref[field, 40 * i + 8 * node : 40 * i + 8 * node + 8, :] for i in range(5)])

    def face_copy(step, number, direction):
        return pltpu.make_async_remote_copy(
            src_ref=face_out.at[step, direction, number],
            dst_ref=face_in.at[step, direction, number],
            send_sem=h_send.at[step, direction],
            recv_sem=h_recv.at[step, direction, number],
            device_id=layer(1 - 2 * direction),
            device_id_type=MESH,
        )

    def face_do(step, number, direction, work):
        @pl.when(has_above if direction == 0 else has_below)
        def _():
            work(face_copy(step, number, direction))

    def face_wait(step, number, direction):
        @pl.when(has_below if direction == 0 else has_above)
        def _():
            face_copy(step, number, direction).wait_recv()

    def pack_two(first, second, direction):
        mask = bit_mask(first.shape, 0)
        if direction == 0:
            return jnp.where(mask, second, lane_roll(first, -1))
        return jnp.where(mask, lane_roll(first, 1), second)

    def near_planes(ref):
        out = []
        for field in range(4):
            low, high = face_rows(ref, field, 1, 0), face_rows(ref, field, 1, 1)
            out.append(jnp.where(bit_mask(low.shape, 0), high, low))
        return out

    def send_planes(step, number, planes):
        for direction in range(2):
            for half, (one, two) in enumerate(((0, 2), (1, 3))):
                packed = pack_two(planes[one], planes[two], direction)
                for line in range(5):
                    at = 25 * half + 5 * line
                    face_out[step, direction, number, at : at + 8, :] = packed[line]
            if number == 0:
                extra = jnp.where(
                    sub == 5,
                    pack_two(coef[BULK], coef[BUOY], direction),
                    pack_two(coef[ACTIVE], coef[ACTIVE], direction),
                )
                face_out[step, direction, number, 48:56, :] = jnp.where(
                    sub >= 5, extra, face_out[step, direction, number, 48:56, :]
                )
            face_do(step, number, direction, start)

    def unpack_two(below, above):
        mask = bit_mask(below.shape, 0)
        return jnp.where(mask, above, below), flip(jnp.where(mask, below, above), 0)

    def arrived_planes(step, number):
        for direction in range(2):
            face_wait(step, number, direction)
        out = []
        for half in range(2):
            rows = [
                jnp.stack(
                    [
                        face_in[step, direction, number, 25 * half + 5 * line : 25 * half + 5 * line + 8, :]
                        for line in range(5)
                    ]
                )
                for direction in range(2)
            ]
            out.append(unpack_two(rows[0], rows[1]))
        return [out[0][0], out[1][0], out[0][1], out[1][1]]

    coef[BULK] = bulk_l
    coef[BUOY] = buoy_l
    coef[ACTIVE] = active
    send_planes(0, 0, near_planes(state.at[0]))

    def element_coefs(at, bulk_e, buoy_e, active_e):
        speed_e = jnp.sqrt(bulk_e * buoy_e)
        use = active_e * k_mask
        coef[at + VOL] = buoy_e * use
        coef[at + VOL + 1] = bulk_e * use
        coef[at + VOL + 2] = GRAVITY / buoy_e * use
        for number, (axis, place) in enumerate(((0, strike), (2, depth))):
            for side in range(2):
                inside = jnp.where(place > 0.5, 1.0, 0.0) if side == 0 else jnp.where(place < 6.5, 1.0, 0.0)
                sign = 1.0 if side == 1 else -1.0
                scale = 5.0 * (use if axis == 0 else active_e)
                jump = scale * jnp.maximum(speed_e, inside * neighbour_lanes(speed_e, axis, side))
                to = at + FACES + 8 * number + 4 * side
                coef[to] = jump
                coef[to + 1] = jump * inside
                coef[to + 2] = sign * scale * inside * neighbour_lanes(buoy_e, axis, side)
                coef[to + 3] = sign * scale * inside * neighbour_lanes(bulk_e, axis, side)
        return speed_e

    speed_l = element_coefs(0, bulk_l, buoy_l, active)
    coef[SPEED] = speed_l
    coef[SELECT] = jnp.where(depth == layers_l - 1.0, 1.0, 0.0)
    for side in range(2):
        use = 5.0 * act_k * (bits[0] if side == 0 else 1.0 - bits[0])
        sign = 1.0 if side == 1 else -1.0
        at = INNER + 3 * side
        coef[at] = use * jnp.maximum(speed_l, neighbour_lanes(speed_l, 1, side))
        coef[at + 1] = sign * use * neighbour_lanes(buoy_l, 1, side)
        coef[at + 2] = sign * use * neighbour_lanes(bulk_l, 1, side)

    def outer_coefs():
        packed = [
            [jnp.broadcast_to(face_in[0, direction, 0, at : at + 1, :], (8, 128)) for direction in range(2)]
            for at in (53, 54)
        ]
        bulk_o, buoy_o = unpack_two(packed[0][0], packed[0][1])
        active_o = unpack_two(packed[1][0], packed[1][1])[0]
        has_low = jnp.where(zc == 0, 0.0, 1.0).astype(jnp.float32)
        has_high = jnp.where(zc == N_ZC - 1, 0.0, 1.0).astype(jnp.float32)
        inside = has_low * (1.0 - bits[0]) + has_high * bits[0]
        buoy_o = buoy_o + (1.0 - inside)
        speed_o = element_coefs(GHOST, bulk_o, buoy_o, active_o)
        sign = 2.0 * bits[0] - 1.0
        speed = jnp.maximum(coef[SPEED], inside * speed_o)
        use = 5.0 * coef[ACTIVE] * k_mask
        coef[OUTER] = use * speed
        coef[OUTER + 1] = use * speed * inside
        coef[OUTER + 2] = use * sign * inside * buoy_o
        coef[OUTER + 3] = use * sign * inside * bulk_o
        use_o = 5.0 * active_o * k_mask * inside
        coef[INTO] = use_o * speed
        coef[INTO + 1] = use_o * speed
        coef[INTO + 2] = -sign * use_o * coef[BUOY]
        coef[INTO + 3] = -sign * use_o * coef[BULK]
        coef[INTO + 4] = KAPPA * bulk_o * buoy_o * active_o * k_mask

    def row(index):
        return coef[index, 0:1, :]

    def rates(src, dst, planes, base):
        def cube(field):
            return src[field].reshape(5, planes, 8, 128)

        def along_i(value):
            return jnp.stack([weighted(TABLE[i], [value[m] for m in range(5)]) for i in range(5)])

        def along_j(value):
            return jnp.stack(
                [weighted(TABLE[j], [value[:, m] for m in range(5)]) for j in range(5)], axis=1
            )

        def along_k(value):
            total = None
            for node in range(5):
                one = jnp.broadcast_to(value[:, :, node : node + 1, :], value.shape)
                term = coef[COL_D + node] * one
                total = term if total is None else total + term
            return total

        def put(field, value):
            dst[field] = value.reshape(40 * planes, 128)

        vol_b, vol_k, vol_g = coef[base + VOL], coef[base + VOL + 1], coef[base + VOL + 2]
        pressure = cube(0)
        put(1, vol_k * along_i(pressure))
        put(2, vol_k * along_j(pressure) if planes == 5 else jnp.zeros_like(pressure))
        put(3, vol_k * along_k(pressure) + vol_g * pressure)
        total = along_i(cube(1)) + along_k(cube(3))
        if planes == 5:
            total = total + along_j(cube(2))
        put(0, vol_b * total)

        size = 8 * planes

        def x_face(ref, field, side):
            return ref[field, 4 * size * side : 4 * size * side + size, :].reshape(planes, 8, 128)

        for side in range(2):
            at = base + FACES + 4 * side
            outer = [neighbour_lanes(x_face(src, field, 1 - side), 0, side) for field in range(4)]
            for field in range(4):
                add = coef[at + 1] * outer[field] - coef[at] * x_face(src, field, side)
                if field == 0:
                    add = add + coef[at + 2] * outer[1]
                if field == 1:
                    add = add + coef[at + 3] * outer[0]
                rows = slice(4 * size * side, 4 * size * side + size)
                dst[field, rows, :] = dst[field, rows, :] + add.reshape(size, 128)

        if planes == 5:
            for side in range(2):
                at = INNER + 3 * side
                outer = [neighbour_lanes(face_rows(src, field, 1, 1 - side), 1, side) for field in range(4)]
                for field in range(4):
                    add = coef[at] * (outer[field] - face_rows(src, field, 1, side))
                    if field == 0:
                        add = add + coef[at + 1] * outer[2]
                    if field == 2:
                        add = add + coef[at + 2] * outer[0]
                    for i in range(5):
                        rows = slice(40 * i + 32 * side, 40 * i + 32 * side + 8)
                        dst[field, rows, :] = dst[field, rows, :] + add[i]

        lines = [[src[field, pl.ds(4 * side, 5 * planes, stride=8), :] for field in range(4)] for side in range(2)]
        for side in range(2):
            at = base + FACES + 8 + 4 * side
            outer = [neighbour_lanes(lines[1 - side][field], 2, side) for field in range(4)]
            for field in range(4):
                add = row(at + 1) * outer[field] - row(at) * lines[side][field]
                if field == 0:
                    add = add + row(at + 2) * outer[3]
                if field == 3:
                    add = add + row(at + 3) * outer[0]
                where = pl.ds(4 * side, 5 * planes, stride=8)
                dst[field, where, :] = dst[field, where, :] + add

    def flux(at, other, own):
        out = [coef[at + 1] * other[field] - coef[at] * own[field] for field in range(4)]
        out[0] = out[0] + coef[at + 2] * other[2]
        out[2] = out[2] + coef[at + 3] * other[0]
        return out

    def add_outer(ref, adds, scale):
        for field in range(4):
            add = scale * adds[field]
            mask = bit_mask(add.shape, 0)
            low, high = jnp.where(mask, 0.0, add), jnp.where(mask, add, 0.0)
            for i in range(5):
                for part, at in ((low, 40 * i), (high, 40 * i + 32)):
                    ref[field, at : at + 8, :] = ref[field, at : at + 8, :] + part[i]

    def add_floor(ref, share):
        for field in range(4):
            floor[field] += share * ref[field, pl.ds(4, 25, stride=8), :]

    def trace_copy(steps, labels=False):
        part = 2 * (steps - 1) + (1 if labels else 0)
        return pltpu.make_async_remote_copy(
            src_ref=label_out if labels else tr_out,
            dst_ref=(label_in if labels else tr_in).at[steps - 1],
            send_sem=t_send.at[part],
            recv_sem=t_recv.at[part],
            device_id=layer(steps),
            device_id_type=MESH,
        )

    def send_floor():
        chosen = [floor[field] * row(SELECT) for field in range(4)]
        pair = [fold_pair(chosen[0], chosen[1], 1), fold_pair(chosen[2], chosen[3], 1)]
        together = fold_pair(pair[0], pair[1], 2)
        tr_out[0:25] = together + flip(together, 5)
        tr_out[25:32] = jnp.zeros((7, 128), jnp.float32)
        for steps in (1, 2):
            trace_copy(steps).start()

    def as_planes(ref):
        return [ref[field].reshape(5, 8, 128) for field in range(4)]

    def put_planes(ref, planes):
        for field in range(4):
            ref[field] = planes[field].reshape(40, 128)

    half, sixth, third = DT / 2.0, DT / 6.0, DT / 3.0
    now, first, second, third_in = state.at[0], state.at[1], state.at[2], state.at[3]

    def time_step(step, carry):
        add_floor(now, sixth)
        rates(now, rate, 5, 0)
        for field in range(4):
            first[field] = now[field] + half * rate[field]
        send_planes(step, 1, near_planes(first))
        rates(first, rate, 5, 0)
        for field in range(4):
            second[field] = now[field] + half * rate[field]
        planes = near_planes(second)
        send_planes(step, 2, planes)
        put_planes(near, planes)
        rates(near, ghost_rate, 1, 0)

        def across(field):
            value = second[field].reshape(5, 5, 8, 128)
            parts = [value[:, m] for m in range(5)]
            low, high = weighted(TABLE[0], parts), weighted(TABLE[4], parts)
            return jnp.where(bit_mask(low.shape, 0), high, low)

        slopes = as_planes(ghost_rate)
        slopes[0] = slopes[0] + coef[VOL] * across(2)
        slopes[2] = slopes[2] + coef[VOL + 1] * across(0)
        starts = near_planes(now)
        send_planes(step, 3, [starts[field] + DT * slopes[field] for field in range(4)])

        outer = arrived_planes(step, 0)

        @pl.when(step == 0)
        def _():
            outer_coefs()
            label_out[...] = wide(nat[1, 125:126])
            for steps in (1, 2):
                trace_copy(steps, True).start()

        own = near_planes(now)
        adds = flux(OUTER, outer, own)
        add_outer(first, adds, half)
        answer = [half * term for term in flux(INTO, own, outer)]
        put_planes(ghost.at[0], answer)

        add_floor(first, third)
        own = near_planes(first)
        came = [half * add for add in adds]
        put_planes(near, came)
        rates(near, ghost_rate, 1, 0)
        slopes = as_planes(ghost_rate)
        for field, source, scale in ((0, 2, coef[VOL]), (2, 0, coef[VOL + 1])):
            inward = scale * came[source]
            for j in range(5):
                weight = jnp.where((lane & 1) != 0, float(TABLE[j, 4]), float(TABLE[j, 0]))
                term = weight * inward
                for i in range(5):
                    at = 40 * i + 8 * j
                    second[field, at : at + 8, :] = second[field, at : at + 8, :] + half * term[i]
        rates(ghost.at[0], ghost_rate, 1, GHOST)
        answered = as_planes(ghost_rate)
        free = arrived_planes(step, 1)
        outer = [free[field] + answer[field] for field in range(4)]
        adds = [slopes[field] + term for field, term in enumerate(flux(OUTER, outer, own))]
        add_outer(second, adds, half)
        answer = [half * (answered[field] + term) for field, term in enumerate(flux(INTO, own, outer))]
        put_planes(ghost.at[1], answer)

        add_floor(second, third)
        rates(second, rate, 5, 0)
        rates(ghost.at[1], ghost_rate, 1, GHOST)
        answered = as_planes(ghost_rate)
        for field in range(4):
            third_in[field] = now[field] + DT * rate[field]
        own = near_planes(second)
        early = as_planes(ghost.at[0])
        for field in (0, 2):
            answered[field] = answered[field] + half * (coef[INTO + 4] * early[field])
        free = arrived_planes(step, 2)
        outer = [free[field] + term for field, term in enumerate(as_planes(ghost.at[1]))]
        adds = flux(OUTER, outer, own)
        add_outer(third_in, adds, DT)
        answer = [DT * (answered[field] + term) for field, term in enumerate(flux(INTO, own, outer))]

        add_floor(third_in, sixth)

        @pl.when(step == STEPS - 1)
        def _():
            send_floor()

        rates(third_in, rate, 5, 0)
        free = arrived_planes(step, 3)
        outer = [free[field] + answer[field] for field in range(4)]
        adds = flux(OUTER, outer, near_planes(third_in))
        for field in range(4):
            inputs = (first[field] - now[field]) + 2.0 * second[field] + third_in[field]
            now[field] = (1.0 / 3.0) * inputs + sixth * rate[field]
        add_outer(now, adds, sixth)

        @pl.when(step < STEPS - 1)
        def _():
            send_planes(step + 1, 0, near_planes(now))

        return carry

    lax.fori_loop(0, STEPS, time_step, 0)

    for line in range(25):
        nat[:, 5 * line : 5 * line + 8, :] = now[:, 8 * line : 8 * line + 8, :]
    back_out[...] = swap_bits(blocks_of(nat), 5).reshape(32, 16, 128)
    back = (back_out, back_in, b_send, b_recv)
    swap_start(*back)
    back_in[me] = back_out[me]

    for steps in (1, 2):
        trace_copy(steps, True).wait_recv()
    from_lane = lax.broadcasted_iota(jnp.int32, (128, 128), 0)
    to_lane = lax.broadcasted_iota(jnp.int32, (128, 128), 1)
    same_field = ((from_lane // 2) % 4 == to_lane // 32) & ((from_lane // 32) % 2 == 0)
    for at, source in enumerate((label_out, label_in.at[0], label_in.at[1])):
        label = jnp.transpose(jnp.broadcast_to(source[0:1], (128, 128))).astype(jnp.int32)
        for upper in range(2):
            owner = (upper * 2 + (to_lane // 2) % 2) * (2 * N_ZC) + 2 * zc + to_lane % 2
            cell = owner * S_DEV + (to_lane // 4) % 8
            chosen[128 * at : 128 * at + 128, 128 * upper : 128 * upper + 128] = jnp.where(
                same_field & (label == cell), 1.0, 0.0
            ).astype(jnp.bfloat16)
    for steps in (1, 2):
        trace_copy(steps).wait_recv()
    rest = jnp.concatenate([tr_out[...], tr_in[0], tr_in[1]], axis=1)
    thirds = []
    for _ in range(3):
        thirds.append(rest.astype(jnp.bfloat16))
        rest = rest - thirds[-1].astype(jnp.float32)
    total = jnp.dot(jnp.concatenate(thirds, axis=0), chosen[...], preferred_element_type=jnp.float32)
    total = total[0:32] + (total[32:64] + total[64:96])
    for upper in range(2):
        part = total[:, 128 * upper : 128 * upper + 128]
        tb_out[4 * upper : 4 * upper + 4] = swap_bits(part.reshape(4, 8, 128), 2)
    ends = (tb_out, tb_in, c_send, c_recv, True)
    swap_start(*ends)
    tb_in[me] = tb_out[gx * 2 + y_lo]

    swap_whole(*back).wait_recv()
    put_blocks(nat, swap_bits(back_in[...].reshape(32, 2, 8, 128), 5))
    elements = field_swap([nat[field, 0:125] for field in range(4)])
    for e in range(4):
        out[e // 2, 0, :, e % 2, :] = elements[e]

    swap_whole(*ends).wait_recv()
    sums = swap_bits(tb_in[...], 5).reshape(8, 32, 128)
    for cell in range(S_DEV):
        trace[pl.ds(cell, 25, stride=8), :] = sums[cell, 0:25]

    for swap in (into, back, ends):
        swap_whole(*swap).wait_send()
    for steps in (1, 2):
        trace_copy(steps).wait_send()
        trace_copy(steps, True).wait_send()

    def drain(step, carry):
        for direction in range(2):
            sent = face_out.at[step, direction]

            @pl.when(has_above if direction == 0 else has_below)
            def _():
                pltpu.make_async_remote_copy(
                    src_ref=sent,
                    dst_ref=face_in.at[step, direction],
                    send_sem=h_send.at[step, direction],
                    recv_sem=h_recv.at[step, direction, 0],
                    device_id=layer(1 - 2 * direction),
                    device_id_type=MESH,
                ).wait_send()

        return carry

    lax.fori_loop(0, STEPS, drain, 0)


def shards(adjoint_state, bulk_modulus, buoyancy, water_layers, surface_cell):
    f32 = jnp.float32
    in_any = pl.BlockSpec(memory_space=pl.ANY)
    dma = pltpu.SemaphoreType.DMA
    by_node = jnp.transpose(adjoint_state, (0, 1, 3, 2, 4))
    in_hbm = [
        pltpu.with_memory_space_constraint(value, pltpu.HBM)
        for value in (by_node, bulk_modulus, buoyancy, water_layers.T, surface_cell.T)
    ]
    out, trace = pl.pallas_call(
        kernel,
        out_shape=(
            jax.ShapeDtypeStruct(by_node.shape, f32),
            jax.ShapeDtypeStruct((S_DEV * 25, 128), f32),
        ),
        in_specs=[in_any] * 5,
        out_specs=(pl.BlockSpec(memory_space=pltpu.VMEM),) * 2,
        scratch_shapes=[
            pltpu.SMEM(bulk_modulus.shape, f32),
            pltpu.SMEM(buoyancy.shape, f32),
            pltpu.SMEM(water_layers.T.shape, jnp.int32),
            pltpu.SMEM(surface_cell.T.shape, jnp.int32),
            pltpu.VMEM(by_node.shape, f32),
            pltpu.VMEM((4, 128, 128), f32),
            pltpu.VMEM((32, 16, 128), f32),
            pltpu.VMEM((32, 16, 128), f32),
            pltpu.VMEM((32, 16, 128), f32),
            pltpu.VMEM((32, 16, 128), f32),
            pltpu.VMEM((4, 4, 200, 128), f32),
            pltpu.VMEM((4, 200, 128), f32),
            pltpu.VMEM((N_COEF, 8, 128), f32),
            pltpu.VMEM((4, 40, 128), f32),
            pltpu.VMEM((2, 4, 40, 128), f32),
            pltpu.VMEM((4, 40, 128), f32),
            pltpu.VMEM((STEPS, 2, 4, 56, 128), f32),
            pltpu.VMEM((STEPS, 2, 4, 56, 128), f32),
            pltpu.VMEM((4, 25, 128), f32),
            pltpu.VMEM((32, 128), f32),
            pltpu.VMEM((2, 32, 128), f32),
            pltpu.VMEM((8, 128), f32),
            pltpu.VMEM((2, 8, 128), f32),
            pltpu.VMEM((384, 256), jnp.bfloat16),
            pltpu.VMEM((8, 8, 128), f32),
            pltpu.VMEM((32, 8, 128), f32),
            dma((5,)),
            dma,
            dma,
            dma((STEPS, 2)),
            dma((STEPS, 2, 4)),
            dma((4,)),
            dma((4,)),
            dma,
            dma,
            dma,
            dma,
        ],
        compiler_params=pltpu.CompilerParams(
            collective_id=0, has_side_effects=True, vmem_limit_bytes=32 * 1024 * 1024
        ),
        name="adjoint_steps",
    )(*in_hbm)
    return (
        jnp.transpose(out, (0, 1, 3, 2, 4)),
        jnp.transpose(trace.reshape(25, S_DEV, 128), (1, 0, 2)),
    )


def solution(mesh):
    placed = (
        P("gx", "gy", "gz", None, None),
        P("gx", "gy", "gz"),
        P("gx", "gy", "gz"),
        P("gx", "gy"),
        P("gx", "gy"),
    )
    return jax.shard_map(
        shards,
        mesh=mesh,
        in_specs=placed,
        out_specs=(P("gx", "gy", "gz", None, None), P(("gx", "gy"), None, None)),
        check_vma=False,
    )
```

```python
import math

import jax
import jax.numpy as jnp
import numpy as np
from jax import lax
from jax.experimental import pallas as pl
from jax.experimental.pallas import tpu as pltpu
from jax.sharding import PartitionSpec as P

N_ZC = 8
RANKS = 32
STEPS = 2
S_DEV = 8
GRAVITY = 2.0
DT = 0.02
MESH = pl.DeviceIdType.MESH


def derivative_rows():
    points = np.array([-1.0, -math.sqrt(3.0 / 7.0), 0.0, math.sqrt(3.0 / 7.0), 1.0])
    scales = np.array(
        [np.prod([points[a] - points[b] for b in range(5) if b != a]) for a in range(5)]
    )
    table = np.zeros((5, 5))
    for a in range(5):
        for b in range(5):
            if a != b:
                table[a, b] = scales[a] / scales[b] / (points[a] - points[b])
        table[a, a] = -np.sum(table[a])
    table[0, 0] += 5.0
    table[4, 4] -= 5.0
    table[np.abs(table) < 1e-12] = 0.0
    return table


TABLE = derivative_rows()
KAPPA = float(np.dot(TABLE[0], TABLE[:, 0]))


def weighted(row, parts):
    total = None
    for weight, part in zip(row, parts):
        if weight != 0.0:
            term = float(weight) * part
            total = term if total is None else total + term
    return total


def bit_mask(shape, bit):
    lanes = lax.broadcasted_iota(jnp.int32, shape, len(shape) - 1)
    return (lanes & (1 << bit)) != 0


def lane_roll(value, shift):
    return pltpu.roll(value, shift % 128, axis=value.ndim - 1)


def swap_pair(low, high, bit):
    width = 1 << bit
    mask = bit_mask(low.shape, bit)
    return (
        jnp.where(mask, lane_roll(high, width), low),
        jnp.where(mask, high, lane_roll(low, -width)),
    )


def swap_stage(value, index_bit, lane_bit):
    step = 1 << index_bit
    shape = value.shape
    split = value.reshape((shape[0] // (2 * step), 2, step) + shape[1:])
    part = split[:, 0].shape
    flat = (-1,) + shape[-2:]
    low, high = swap_pair(split[:, 0].reshape(flat), split[:, 1].reshape(flat), lane_bit)
    return jnp.stack([low.reshape(part), high.reshape(part)], axis=1).reshape(shape)


def swap_bits(value, count):
    for bit in range(count):
        value = swap_stage(value, bit, bit)
    return value


def flip(value, bit):
    width = 1 << bit
    mask = bit_mask(value.shape, bit)
    return jnp.where(mask, lane_roll(value, width), lane_roll(value, -width))


def fold_pair(low, high, bit):
    mask = bit_mask(low.shape, bit)
    return jnp.where(mask, high, low) + flip(jnp.where(mask, low, high), bit)


def neighbour_lanes(value, axis, side):
    if axis == 1:
        return lane_roll(value, 1 if side == 0 else -1)
    wide, short, bit = (64, 56, 6) if axis == 0 else (32, 30, 5)
    mask = bit_mask(value.shape, bit)
    if side == 0:
        return jnp.where(mask, lane_roll(value, wide), lane_roll(value, -short))
    return jnp.where(mask, lane_roll(value, short), lane_roll(value, -wide))


def hops(turn, mask):
    return min(turn, 4 - turn) + {0: 0, 1: 1, 4: 2, 5: 1}[mask & 5]


FAR_FIRST = sorted(
    ((turn, mask) for turn in range(4) for mask in range(8) if turn or mask),
    key=lambda pair: (-hops(*pair), pair[1] & 5, pair[0]),
)

VOL = 0
FACES = 3
SET = 19
GHOST = SET
INNER = 2 * SET
OUTER = INNER + 6
INTO = OUTER + 4
COL_D = INTO + 5
SELECT = COL_D + 5
BULK, BUOY, ACTIVE, SPEED = SELECT + 1, SELECT + 2, SELECT + 3, SELECT + 4
N_COEF = SPEED + 1


def kernel(
    state_hbm, bulk_hbm, buoy_hbm, layers_hbm, cells_hbm, out, trace,
    bulk, buoy, layers, cells,
    staged, nat, pack_out, pack_in, back_out, back_in, state, rate, coef,
    near, ghost, ghost_rate, face_out, face_in, floor, tr_out, tr_in, label_out, label_in, chosen, tb_out, tb_in, sums_out,
    local_sem, a_send, a_recv, h_send, h_recv, t_send, t_recv, b_send, b_recv, c_send, c_recv,
):
    gx = lax.axis_index("gx")
    gy = lax.axis_index("gy")
    gz = lax.axis_index("gz")
    zc, y_lo = gy // 2, gy % 2
    me = gx * 8 + gz * 2 + y_lo

    load = pltpu.make_async_copy(state_hbm, staged.at[pl.ds(0, 2)], local_sem.at[0])
    load.start()
    small = [
        pltpu.make_async_copy(source, target, local_sem.at[1 + at])
        for at, (source, target) in enumerate(
            ((bulk_hbm, bulk), (buoy_hbm, buoy), (layers_hbm, layers), (cells_hbm, cells))
        )
    ]
    for copy in small:
        copy.start()

    def device_of(rank):
        return (rank // 8, zc * 2 + rank % 2, (rank // 2) % 4)

    def layer(steps):
        return (gx, (gy + 2 * steps + 2 * N_ZC) % (2 * N_ZC), gz)

    barrier = pltpu.get_barrier_semaphore()

    has_below, has_above = zc > 0, zc < N_ZC - 1

    def greet(device):
        pl.semaphore_signal(barrier, inc=1, device_id=device, device_id_type=MESH)

    for delta in range(1, RANKS):
        greet(device_of((me + delta) % RANKS))

    @pl.when(has_below)
    def _():
        greet(layer(-1))

    @pl.when(has_above)
    def _():
        greet(layer(1))

    @pl.when(zc == 0)
    def _():
        greet(layer(-1))
        greet(layer(-2))

    @pl.when(zc == 1)
    def _():
        greet(layer(-2))

    greetings = (
        RANKS - 1
        + has_below.astype(jnp.int32)
        + has_above.astype(jnp.int32)
        + (zc == N_ZC - 2).astype(jnp.int32)
        + 2 * (zc == N_ZC - 1).astype(jnp.int32)
    )

    floor[...] = jnp.zeros_like(floor)
    face_out[...] = jnp.zeros_like(face_out)

    @pl.when(zc == 0)
    def _():
        face_in[:, 0] = jnp.zeros((STEPS, 4, 56, 128), jnp.float32)

    @pl.when(zc == N_ZC - 1)
    def _():
        face_in[:, 1] = jnp.zeros((STEPS, 4, 56, 128), jnp.float32)

    sub = lax.broadcasted_iota(jnp.int32, (8, 128), 0)
    lane = lax.broadcasted_iota(jnp.int32, (8, 128), 1)
    bits = [jnp.where((lane & (1 << bit)) != 0, 1.0, 0.0) for bit in range(7)]
    k_mask = jnp.where(sub < 5, 1.0, 0.0)
    for node in range(5):
        column = jnp.zeros((8, 128), jnp.float32)
        for row_at in range(5):
            if TABLE[row_at, node] != 0.0:
                column = jnp.where(sub == row_at, float(TABLE[row_at, node]), column)
        coef[COL_D + node] = column

    lane1 = lax.broadcasted_iota(jnp.int32, (1, 128), 1)
    high1 = (lane1 & 64) != 0
    low1 = (lane1 & 32) != 0

    def element_row(ref):
        return jnp.where(
            high1,
            jnp.where(low1, ref[1, 0, 1], ref[1, 0, 0]),
            jnp.where(low1, ref[0, 0, 1], ref[0, 0, 0]),
        )

    def column_row(ref):
        return jnp.where(high1, ref[0, 1].astype(jnp.float32), ref[0, 0].astype(jnp.float32))

    def blocks_of(ref):
        return jnp.stack(
            [
                jnp.stack([ref[low, 8 * tile : 8 * tile + 8], ref[2 + low, 8 * tile : 8 * tile + 8]])
                for tile in range(16)
                for low in range(2)
            ]
        )

    def put_blocks(ref, value):
        for at in range(32):
            tile, low = at // 2, at % 2
            for high in range(2):
                ref[2 * high + low, 8 * tile : 8 * tile + 8] = value[at, high]

    def field_swap(parts):
        for step, bit in ((1, 5), (2, 6)):
            for at in range(4):
                if not at & step:
                    parts[at], parts[at + step] = swap_pair(parts[at], parts[at + step], bit)
        return parts

    load.wait()
    for copy in small:
        copy.wait()
    fields = field_swap([staged[e // 2, 0, :, e % 2, :] for e in range(4)])
    for field in range(4):
        nat[field, 0:125] = fields[field]
    nat[0, 125:126] = element_row(bulk)
    nat[0, 126:127] = element_row(buoy)
    nat[0, 127:128] = column_row(layers)
    cell_row = column_row(cells)
    nat[1, 125:126] = cell_row
    nat[1, 126:127] = cell_row
    nat[1, 127:128] = cell_row
    for field in (2, 3):
        nat[field, 125:128] = jnp.zeros((3, 128), jnp.float32)
    pack_out[...] = swap_bits(blocks_of(nat), 5).reshape(32, 16, 128)

    pl.semaphore_wait(barrier, greetings)

    def start(copy):
        copy.start()

    def leave(copy):
        copy.wait_send()

    def swap_start(out_ref, in_ref, send, recv, by_owner=False):
        for turn, mask in FAR_FIRST:
            low = [(me // (1 << b)) % 2 for b in range(3)]
            low = [1 - v if mask & (1 << b) else v for b, v in enumerate(low)]
            rank = ((gx + turn) % 4) * 8 + low[2] * 4 + low[1] * 2 + low[0]
            pltpu.make_async_remote_copy(
                src_ref=out_ref.at[(rank // 8) * 2 + rank % 2 if by_owner else rank],
                dst_ref=in_ref.at[me],
                send_sem=send,
                recv_sem=recv,
                device_id=device_of(rank),
                device_id_type=MESH,
            ).start()

    def swap_whole(out_ref, in_ref, send, recv, by_owner=False):
        others = in_ref.at[pl.ds(0, RANKS - 1)]
        return pltpu.make_async_remote_copy(
            src_ref=others,
            dst_ref=others,
            send_sem=send,
            recv_sem=recv,
            device_id=device_of((me + 1) % RANKS),
            device_id_type=MESH,
        )

    into = (pack_out, pack_in, a_send, a_recv)
    swap_start(*into)
    pack_in[me] = pack_out[me]
    swap_whole(*into).wait_recv()
    put_blocks(nat, swap_bits(pack_in[...].reshape(32, 2, 8, 128), 5))

    def wide(row_value):
        return jnp.broadcast_to(row_value, (8, 128))

    bulk_l = wide(nat[0, 125:126])
    buoy_l = wide(nat[0, 126:127])
    layers_l = wide(nat[0, 127:128])
    depth = 4.0 * bits[2] + 2.0 * bits[1] + bits[5]
    strike = 4.0 * bits[4] + 2.0 * bits[3] + bits[6]
    active = jnp.where(depth < layers_l, 1.0, 0.0)
    act_k = active * k_mask

    for line in range(25):
        state[0, :, 8 * line : 8 * line + 8, :] = nat[:, 5 * line : 5 * line + 8, :] * act_k

    def face_rows(ref, field, axis, side):
        node = 4 * side
        if axis == 0:
            return ref[field, 40 * node : 40 * node + 40, :].reshape(5, 8, 128)
        return jnp.stack([ref[field, 40 * i + 8 * node : 40 * i + 8 * node + 8, :] for i in range(5)])

    def face_copy(step, number, direction):
        return pltpu.make_async_remote_copy(
            src_ref=face_out.at[step, direction, number],
            dst_ref=face_in.at[step, direction, number],
            send_sem=h_send.at[step, direction],
            recv_sem=h_recv.at[step, direction, number],
            device_id=layer(1 - 2 * direction),
            device_id_type=MESH,
        )

    def face_do(step, number, direction, work):
        @pl.when(has_above if direction == 0 else has_below)
        def _():
            work(face_copy(step, number, direction))

    def face_wait(step, number, direction):
        @pl.when(has_below if direction == 0 else has_above)
        def _():
            face_copy(step, number, direction).wait_recv()

    def pack_two(first, second, direction):
        mask = bit_mask(first.shape, 0)
        if direction == 0:
            return jnp.where(mask, second, lane_roll(first, -1))
        return jnp.where(mask, lane_roll(first, 1), second)

    def near_planes(ref):
        out = []
        for field in range(4):
            low, high = face_rows(ref, field, 1, 0), face_rows(ref, field, 1, 1)
            out.append(jnp.where(bit_mask(low.shape, 0), high, low))
        return out

    def send_planes(step, number, planes):
        for direction in range(2):
            for half, (one, two) in enumerate(((0, 2), (1, 3))):
                packed = pack_two(planes[one], planes[two], direction)
                for line in range(5):
                    at = 25 * half + 5 * line
                    face_out[step, direction, number, at : at + 8, :] = packed[line]
            if number == 0:
                extra = jnp.where(
                    sub == 5,
                    pack_two(coef[BULK], coef[BUOY], direction),
                    pack_two(coef[ACTIVE], coef[ACTIVE], direction),
                )
                face_out[step, direction, number, 48:56, :] = jnp.where(
                    sub >= 5, extra, face_out[step, direction, number, 48:56, :]
                )
            face_do(step, number, direction, start)

    def unpack_two(below, above):
        mask = bit_mask(below.shape, 0)
        return jnp.where(mask, above, below), flip(jnp.where(mask, below, above), 0)

    def arrived_planes(step, number):
        for direction in range(2):
            face_wait(step, number, direction)
        out = []
        for half in range(2):
            rows = [
                jnp.stack(
                    [
                        face_in[step, direction, number, 25 * half + 5 * line : 25 * half + 5 * line + 8, :]
                        for line in range(5)
                    ]
                )
                for direction in range(2)
            ]
            out.append(unpack_two(rows[0], rows[1]))
        return [out[0][0], out[1][0], out[0][1], out[1][1]]

    coef[BULK] = bulk_l
    coef[BUOY] = buoy_l
    coef[ACTIVE] = active
    send_planes(0, 0, near_planes(state.at[0]))

    def element_coefs(at, bulk_e, buoy_e, active_e):
        speed_e = jnp.sqrt(bulk_e * buoy_e)
        use = active_e * k_mask
        coef[at + VOL] = buoy_e * use
        coef[at + VOL + 1] = bulk_e * use
        coef[at + VOL + 2] = GRAVITY / buoy_e * use
        for number, (axis, place) in enumerate(((0, strike), (2, depth))):
            for side in range(2):
                inside = jnp.where(place > 0.5, 1.0, 0.0) if side == 0 else jnp.where(place < 6.5, 1.0, 0.0)
                sign = 1.0 if side == 1 else -1.0
                scale = 5.0 * (use if axis == 0 else active_e)
                jump = scale * jnp.maximum(speed_e, inside * neighbour_lanes(speed_e, axis, side))
                to = at + FACES + 8 * number + 4 * side
                coef[to] = jump
                coef[to + 1] = jump * inside
                coef[to + 2] = sign * scale * inside * neighbour_lanes(buoy_e, axis, side)
                coef[to + 3] = sign * scale * inside * neighbour_lanes(bulk_e, axis, side)
        return speed_e

    speed_l = element_coefs(0, bulk_l, buoy_l, active)
    coef[SPEED] = speed_l
    coef[SELECT] = jnp.where(depth == layers_l - 1.0, 1.0, 0.0)
    for side in range(2):
        use = 5.0 * act_k * (bits[0] if side == 0 else 1.0 - bits[0])
        sign = 1.0 if side == 1 else -1.0
        at = INNER + 3 * side
        coef[at] = use * jnp.maximum(speed_l, neighbour_lanes(speed_l, 1, side))
        coef[at + 1] = sign * use * neighbour_lanes(buoy_l, 1, side)
        coef[at + 2] = sign * use * neighbour_lanes(bulk_l, 1, side)

    def outer_coefs():
        packed = [
            [jnp.broadcast_to(face_in[0, direction, 0, at : at + 1, :], (8, 128)) for direction in range(2)]
            for at in (53, 54)
        ]
        bulk_o, buoy_o = unpack_two(packed[0][0], packed[0][1])
        active_o = unpack_two(packed[1][0], packed[1][1])[0]
        has_low = jnp.where(zc == 0, 0.0, 1.0).astype(jnp.float32)
        has_high = jnp.where(zc == N_ZC - 1, 0.0, 1.0).astype(jnp.float32)
        inside = has_low * (1.0 - bits[0]) + has_high * bits[0]
        buoy_o = buoy_o + (1.0 - inside)
        speed_o = element_coefs(GHOST, bulk_o, buoy_o, active_o)
        sign = 2.0 * bits[0] - 1.0
        speed = jnp.maximum(coef[SPEED], inside * speed_o)
        use = 5.0 * coef[ACTIVE] * k_mask
        coef[OUTER] = use * speed
        coef[OUTER + 1] = use * speed * inside
        coef[OUTER + 2] = use * sign * inside * buoy_o
        coef[OUTER + 3] = use * sign * inside * bulk_o
        use_o = 5.0 * active_o * k_mask * inside
        coef[INTO] = use_o * speed
        coef[INTO + 1] = use_o * speed
        coef[INTO + 2] = -sign * use_o * coef[BUOY]
        coef[INTO + 3] = -sign * use_o * coef[BULK]
        coef[INTO + 4] = KAPPA * bulk_o * buoy_o * active_o * k_mask

    def row(index):
        return coef[index, 0:1, :]

    def rates(src, dst, planes, base):
        def cube(field):
            return src[field].reshape(5, planes, 8, 128)

        def along_i(value):
            return jnp.stack([weighted(TABLE[i], [value[m] for m in range(5)]) for i in range(5)])

        def along_j(value):
            return jnp.stack(
                [weighted(TABLE[j], [value[:, m] for m in range(5)]) for j in range(5)], axis=1
            )

        def along_k(value):
            total = None
            for node in range(5):
                one = jnp.broadcast_to(value[:, :, node : node + 1, :], value.shape)
                term = coef[COL_D + node] * one
                total = term if total is None else total + term
            return total

        def put(field, value):
            dst[field] = value.reshape(40 * planes, 128)

        vol_b, vol_k, vol_g = coef[base + VOL], coef[base + VOL + 1], coef[base + VOL + 2]
        pressure = cube(0)
        put(1, vol_k * along_i(pressure))
        put(2, vol_k * along_j(pressure) if planes == 5 else jnp.zeros_like(pressure))
        put(3, vol_k * along_k(pressure) + vol_g * pressure)
        total = along_i(cube(1)) + along_k(cube(3))
        if planes == 5:
            total = total + along_j(cube(2))
        put(0, vol_b * total)

        size = 8 * planes

        def x_face(ref, field, side):
            return ref[field, 4 * size * side : 4 * size * side + size, :].reshape(planes, 8, 128)

        for side in range(2):
            at = base + FACES + 4 * side
            outer = [neighbour_lanes(x_face(src, field, 1 - side), 0, side) for field in range(4)]
            for field in range(4):
                add = coef[at + 1] * outer[field] - coef[at] * x_face(src, field, side)
                if field == 0:
                    add = add + coef[at + 2] * outer[1]
                if field == 1:
                    add = add + coef[at + 3] * outer[0]
                rows = slice(4 * size * side, 4 * size * side + size)
                dst[field, rows, :] = dst[field, rows, :] + add.reshape(size, 128)

        if planes == 5:
            for side in range(2):
                at = INNER + 3 * side
                outer = [neighbour_lanes(face_rows(src, field, 1, 1 - side), 1, side) for field in range(4)]
                for field in range(4):
                    add = coef[at] * (outer[field] - face_rows(src, field, 1, side))
                    if field == 0:
                        add = add + coef[at + 1] * outer[2]
                    if field == 2:
                        add = add + coef[at + 2] * outer[0]
                    for i in range(5):
                        rows = slice(40 * i + 32 * side, 40 * i + 32 * side + 8)
                        dst[field, rows, :] = dst[field, rows, :] + add[i]

        lines = [[src[field, pl.ds(4 * side, 5 * planes, stride=8), :] for field in range(4)] for side in range(2)]
        for side in range(2):
            at = base + FACES + 8 + 4 * side
            outer = [neighbour_lanes(lines[1 - side][field], 2, side) for field in range(4)]
            for field in range(4):
                add = row(at + 1) * outer[field] - row(at) * lines[side][field]
                if field == 0:
                    add = add + row(at + 2) * outer[3]
                if field == 3:
                    add = add + row(at + 3) * outer[0]
                where = pl.ds(4 * side, 5 * planes, stride=8)
                dst[field, where, :] = dst[field, where, :] + add

    def flux(at, other, own):
        out = [coef[at + 1] * other[field] - coef[at] * own[field] for field in range(4)]
        out[0] = out[0] + coef[at + 2] * other[2]
        out[2] = out[2] + coef[at + 3] * other[0]
        return out

    def add_outer(ref, adds, scale):
        for field in range(4):
            add = scale * adds[field]
            mask = bit_mask(add.shape, 0)
            low, high = jnp.where(mask, 0.0, add), jnp.where(mask, add, 0.0)
            for i in range(5):
                for part, at in ((low, 40 * i), (high, 40 * i + 32)):
                    ref[field, at : at + 8, :] = ref[field, at : at + 8, :] + part[i]

    def add_floor(ref, share):
        for field in range(4):
            floor[field] += share * ref[field, pl.ds(4, 25, stride=8), :]

    def trace_copy(steps, labels=False):
        part = 2 * (steps - 1) + (1 if labels else 0)
        return pltpu.make_async_remote_copy(
            src_ref=label_out if labels else tr_out,
            dst_ref=(label_in if labels else tr_in).at[steps - 1],
            send_sem=t_send.at[part],
            recv_sem=t_recv.at[part],
            device_id=layer(steps),
            device_id_type=MESH,
        )

    def send_floor():
        chosen = [floor[field] * row(SELECT) for field in range(4)]
        pair = [fold_pair(chosen[0], chosen[1], 1), fold_pair(chosen[2], chosen[3], 1)]
        together = fold_pair(pair[0], pair[1], 2)
        tr_out[0:25] = together + flip(together, 5)
        tr_out[25:32] = jnp.zeros((7, 128), jnp.float32)
        for steps in (1, 2):
            trace_copy(steps).start()

    def as_planes(ref):
        return [ref[field].reshape(5, 8, 128) for field in range(4)]

    def put_planes(ref, planes):
        for field in range(4):
            ref[field] = planes[field].reshape(40, 128)

    half, sixth, third = DT / 2.0, DT / 6.0, DT / 3.0
    now, first, second, third_in = state.at[0], state.at[1], state.at[2], state.at[3]

    def time_step(step, carry):
        add_floor(now, sixth)
        rates(now, rate, 5, 0)
        for field in range(4):
            first[field] = now[field] + half * rate[field]
        send_planes(step, 1, near_planes(first))
        rates(first, rate, 5, 0)
        for field in range(4):
            second[field] = now[field] + half * rate[field]
        planes = near_planes(second)
        send_planes(step, 2, planes)
        put_planes(near, planes)
        rates(near, ghost_rate, 1, 0)

        def across(field):
            value = second[field].reshape(5, 5, 8, 128)
            parts = [value[:, m] for m in range(5)]
            low, high = weighted(TABLE[0], parts), weighted(TABLE[4], parts)
            return jnp.where(bit_mask(low.shape, 0), high, low)

        slopes = as_planes(ghost_rate)
        slopes[0] = slopes[0] + coef[VOL] * across(2)
        slopes[2] = slopes[2] + coef[VOL + 1] * across(0)
        starts = near_planes(now)
        send_planes(step, 3, [starts[field] + DT * slopes[field] for field in range(4)])

        outer = arrived_planes(step, 0)

        @pl.when(step == 0)
        def _():
            outer_coefs()
            label_out[...] = wide(nat[1, 125:126])
            for steps in (1, 2):
                trace_copy(steps, True).start()

        own = near_planes(now)
        adds = flux(OUTER, outer, own)
        add_outer(first, adds, half)
        answer = [half * term for term in flux(INTO, own, outer)]
        put_planes(ghost.at[0], answer)

        add_floor(first, third)
        own = near_planes(first)
        came = [half * add for add in adds]
        put_planes(near, came)
        rates(near, ghost_rate, 1, 0)
        slopes = as_planes(ghost_rate)
        for field, source, scale in ((0, 2, coef[VOL]), (2, 0, coef[VOL + 1])):
            inward = scale * came[source]
            for j in range(5):
                weight = jnp.where((lane & 1) != 0, float(TABLE[j, 4]), float(TABLE[j, 0]))
                term = weight * inward
                for i in range(5):
                    at = 40 * i + 8 * j
                    second[field, at : at + 8, :] = second[field, at : at + 8, :] + half * term[i]
        rates(ghost.at[0], ghost_rate, 1, GHOST)
        answered = as_planes(ghost_rate)
        free = arrived_planes(step, 1)
        outer = [free[field] + answer[field] for field in range(4)]
        adds = [slopes[field] + term for field, term in enumerate(flux(OUTER, outer, own))]
        add_outer(second, adds, half)
        answer = [half * (answered[field] + term) for field, term in enumerate(flux(INTO, own, outer))]
        put_planes(ghost.at[1], answer)

        add_floor(second, third)
        rates(second, rate, 5, 0)
        rates(ghost.at[1], ghost_rate, 1, GHOST)
        answered = as_planes(ghost_rate)
        for field in range(4):
            third_in[field] = now[field] + DT * rate[field]
        own = near_planes(second)
        early = as_planes(ghost.at[0])
        for field in (0, 2):
            answered[field] = answered[field] + half * (coef[INTO + 4] * early[field])
        free = arrived_planes(step, 2)
        outer = [free[field] + term for field, term in enumerate(as_planes(ghost.at[1]))]
        adds = flux(OUTER, outer, own)
        add_outer(third_in, adds, DT)
        answer = [DT * (answered[field] + term) for field, term in enumerate(flux(INTO, own, outer))]

        add_floor(third_in, sixth)

        @pl.when(step == STEPS - 1)
        def _():
            send_floor()

        rates(third_in, rate, 5, 0)
        free = arrived_planes(step, 3)
        outer = [free[field] + answer[field] for field in range(4)]
        adds = flux(OUTER, outer, near_planes(third_in))
        for field in range(4):
            inputs = (first[field] - now[field]) + 2.0 * second[field] + third_in[field]
            now[field] = (1.0 / 3.0) * inputs + sixth * rate[field]
        add_outer(now, adds, sixth)

        @pl.when(step < STEPS - 1)
        def _():
            send_planes(step + 1, 0, near_planes(now))

        return carry

    lax.fori_loop(0, STEPS, time_step, 0)

    for line in range(25):
        nat[:, 5 * line : 5 * line + 8, :] = now[:, 8 * line : 8 * line + 8, :]
    back_out[...] = swap_bits(blocks_of(nat), 5).reshape(32, 16, 128)
    back = (back_out, back_in, b_send, b_recv)
    swap_start(*back)
    back_in[me] = back_out[me]

    for steps in (1, 2):
        trace_copy(steps, True).wait_recv()
    from_lane = lax.broadcasted_iota(jnp.int32, (128, 128), 0)
    to_lane = lax.broadcasted_iota(jnp.int32, (128, 128), 1)
    same_field = ((from_lane // 2) % 4 == to_lane // 32) & ((from_lane // 32) % 2 == 0)
    for at, source in enumerate((label_out, label_in.at[0], label_in.at[1])):
        label = jnp.transpose(jnp.broadcast_to(source[0:1], (128, 128))).astype(jnp.int32)
        for upper in range(2):
            owner = (upper * 2 + (to_lane // 2) % 2) * (2 * N_ZC) + 2 * zc + to_lane % 2
            cell = owner * S_DEV + (to_lane // 4) % 8
            chosen[128 * at : 128 * at + 128, 128 * upper : 128 * upper + 128] = jnp.where(
                same_field & (label == cell), 1.0, 0.0
            ).astype(jnp.bfloat16)
    for steps in (1, 2):
        trace_copy(steps).wait_recv()
    rest = jnp.concatenate([tr_out[...], tr_in[0], tr_in[1]], axis=1)
    thirds = []
    for _ in range(3):
        thirds.append(rest.astype(jnp.bfloat16))
        rest = rest - thirds[-1].astype(jnp.float32)
    total = jnp.dot(jnp.concatenate(thirds, axis=0), chosen[...], preferred_element_type=jnp.float32)
    total = total[0:32] + (total[32:64] + total[64:96])
    for upper in range(2):
        part = total[:, 128 * upper : 128 * upper + 128]
        tb_out[4 * upper : 4 * upper + 4] = swap_bits(part.reshape(4, 8, 128), 2)
    ends = (tb_out, tb_in, c_send, c_recv, True)
    swap_start(*ends)
    tb_in[me] = tb_out[gx * 2 + y_lo]

    swap_whole(*back).wait_recv()
    put_blocks(nat, swap_bits(back_in[...].reshape(32, 2, 8, 128), 5))
    elements = field_swap([nat[field, 0:125] for field in range(4)])
    for e in range(4):
        staged[e // 2, 0, :, e % 2, :] = elements[e]

    store = pltpu.make_async_copy(staged.at[pl.ds(0, 2)], out, local_sem.at[5])
    store.start()

    swap_whole(*ends).wait_recv()
    sums = swap_bits(tb_in[...], 5).reshape(8, 32, 128)
    for cell in range(S_DEV):
        sums_out[pl.ds(cell, 25, stride=8), :] = sums[cell, 0:25]
    store_trace = pltpu.make_async_copy(sums_out.at[pl.ds(0, 8 * 25)], trace, local_sem.at[6])
    store_trace.start()

    for swap in (into, back, ends):
        swap_whole(*swap).wait_send()
    for steps in (1, 2):
        trace_copy(steps).wait_send()
        trace_copy(steps, True).wait_send()

    def drain(step, carry):
        for direction in range(2):
            sent = face_out.at[step, direction]

            @pl.when(has_above if direction == 0 else has_below)
            def _():
                pltpu.make_async_remote_copy(
                    src_ref=sent,
                    dst_ref=face_in.at[step, direction],
                    send_sem=h_send.at[step, direction],
                    recv_sem=h_recv.at[step, direction, 0],
                    device_id=layer(1 - 2 * direction),
                    device_id_type=MESH,
                ).wait_send()

        return carry

    lax.fori_loop(0, STEPS, drain, 0)
    store.wait()
    store_trace.wait()


def shards(adjoint_state, bulk_modulus, buoyancy, water_layers, surface_cell):
    f32 = jnp.float32
    in_any = pl.BlockSpec(memory_space=pl.ANY)
    dma = pltpu.SemaphoreType.DMA
    by_node = jnp.transpose(adjoint_state, (0, 1, 3, 2, 4))
    in_hbm = [
        pltpu.with_memory_space_constraint(value, pltpu.HBM)
        for value in (by_node, bulk_modulus, buoyancy, water_layers.T, surface_cell.T)
    ]
    out, trace = pl.pallas_call(
        kernel,
        out_shape=(
            jax.ShapeDtypeStruct(by_node.shape, f32),
            jax.ShapeDtypeStruct((S_DEV * 25, 128), f32),
        ),
        in_specs=[in_any] * 5,
        out_specs=(in_any, in_any),
        scratch_shapes=[
            pltpu.SMEM(bulk_modulus.shape, f32),
            pltpu.SMEM(buoyancy.shape, f32),
            pltpu.SMEM(water_layers.T.shape, jnp.int32),
            pltpu.SMEM(surface_cell.T.shape, jnp.int32),
            pltpu.VMEM((3,) + by_node.shape[1:], f32),
            pltpu.VMEM((4, 128, 128), f32),
            pltpu.VMEM((32, 16, 128), f32),
            pltpu.VMEM((32, 16, 128), f32),
            pltpu.VMEM((32, 16, 128), f32),
            pltpu.VMEM((32, 16, 128), f32),
            pltpu.VMEM((5, 4, 200, 128), f32),
            pltpu.VMEM((5, 200, 128), f32),
            pltpu.VMEM((N_COEF, 8, 128), f32),
            pltpu.VMEM((5, 40, 128), f32),
            pltpu.VMEM((3, 4, 40, 128), f32),
            pltpu.VMEM((5, 40, 128), f32),
            pltpu.VMEM((STEPS, 2, 4, 56, 128), f32),
            pltpu.VMEM((STEPS, 2, 4, 56, 128), f32),
            pltpu.VMEM((4, 25, 128), f32),
            pltpu.VMEM((32, 128), f32),
            pltpu.VMEM((2, 32, 128), f32),
            pltpu.VMEM((8, 128), f32),
            pltpu.VMEM((2, 8, 128), f32),
            pltpu.VMEM((384, 256), jnp.bfloat16),
            pltpu.VMEM((8, 8, 128), f32),
            pltpu.VMEM((32, 8, 128), f32),
            pltpu.VMEM((256, 128), f32),
            dma((7,)),
            dma,
            dma,
            dma((STEPS, 2)),
            dma((STEPS, 2, 4)),
            dma((4,)),
            dma((4,)),
            dma,
            dma,
            dma,
            dma,
        ],
        compiler_params=pltpu.CompilerParams(
            collective_id=0, has_side_effects=True, vmem_limit_bytes=32 * 1024 * 1024
        ),
        name="adjoint_steps",
    )(*in_hbm)
    return (
        jnp.transpose(out, (0, 1, 3, 2, 4)),
        jnp.transpose(trace.reshape(25, S_DEV, 128), (1, 0, 2)),
    )


def solution(mesh):
    placed = (
        P("gx", "gy", "gz", None, None),
        P("gx", "gy", "gz"),
        P("gx", "gy", "gz"),
        P("gx", "gy"),
        P("gx", "gy"),
    )
    return jax.shard_map(
        shards,
        mesh=mesh,
        in_specs=placed,
        out_specs=(P("gx", "gy", "gz", None, None), P(("gx", "gy"), None, None)),
        check_vma=False,
    )
```
